256 devices in a mesh: view: 32 (over x, z), row: 4 (over y), dp: 2 (over core).
Axes of the slice: x: 4, y: 4, z: 8, core: 2. Of those that a mesh axis runs over, the one named last changes fastest.
Arguments:
- queries: bfloat16 [2, 32, 1024, 1024], P('dp', 'view', 'row'), may hold values from -16 to 16
- key_tokens: bfloat16 [2, 32, 1024, 1024], P('dp', 'view', 'row'), may hold values from -16 to 16
- values: bfloat16 [2, 32, 1024, 1024], P('dp', 'view', 'row'), may hold values from -6 to 6
- encoder_feats: bfloat16 [2, 32, 1024, 768], P('dp', 'view', 'row'), may hold values from -6 to 6
- proj_weight: bfloat16 [1024, 768], P('view'), may hold values from -0.1875 to 0.1875
- pick_blocks: int32 [2, 32, 4, 8], P('dp', 'view', 'row'), may hold values from 0 to 1
- pair_mask: int32 [2, 32, 8, 8], P('dp', 'view', 'row'), may hold values 0 or 1
- step_ids: int32 [2, 32], P('dp', 'view'), may hold values from 0 to 999
- step_weight: float32 [1000], replicated, may hold values from 2 to 32
Outputs:
- grad_queries: bfloat16 [2, 32, 1024, 1024], P('dp', 'view', 'row')
- grad_keys: bfloat16 [2, 32, 1024, 1024], P('dp', 'view', 'row')
- grad_values: bfloat16 [2, 32, 1024, 1024], P('dp', 'view', 'row')
- grad_proj: float32 [1024, 768], P('view')
The draws below stay inside these ranges and needn't reach their ends.
Inputs may be any that keep to these rules, and one draw needn't show every extreme that they name: pick_blocks[s, j, r, m] is the block of band r of view j that view j - offset_m reads.
All inputs are finite; a program needn't handle non-finite values. No bound on the sum of `pair_mask` on one device may be relied on, other than what follows from the above.
Results may differ from the reference program's by a relative error of at most 0.024.
Values may be sent and summed in bfloat16 or wider, within the bound.
A program may use at most 128 MiB of HBM per device.

```python
import math
import jax
import jax.numpy as jnp
from jax import lax

HEADS = 8
HS = 128
HD = 1024
E = 768
BLK = 128
STEPS = 1000
ROWS_DEV = 256
QB = 2
VROWS = 1024
VIEWS = 32
SCENES = 2
PAIRS = 8
N_ROW = 4


def draw_queries(key, part):
    own_key = jax.random.fold_in(key, 3)
    full_shape = (SCENES, VIEWS, VROWS, HEADS * HS)
    return jax.random.truncated_normal(own_key, -6.0, 6.0, full_shape, jnp.float32).astype(jnp.bfloat16)


def draw_key_tokens(key, part):
    own_key = jax.random.fold_in(key, 7)
    full_shape = (SCENES, VIEWS, VROWS, HEADS * HS)
    return jax.random.truncated_normal(own_key, -6.0, 6.0, full_shape, jnp.float32).astype(jnp.bfloat16)


def touch_ends(drawn, stream_key, least, high):
    longest = drawn.shape.index(max(drawn.shape))
    spots = []
    for shift in (0, 1):
        where = [jax.random.randint(jax.random.fold_in(stream_key, axis), (), 0, length) for axis, length in enumerate(drawn.shape)]
        where[longest] = (where[longest] + shift) % drawn.shape[longest]
        spots.append(tuple(where))
    return drawn.at[spots[0]].set(least).at[spots[1]].set(high)


def steps_of(key, dims, cuts, least, high):
    level, own = 1.0, jax.random.fold_in(key, 6)
    for dim, parts in cuts:
        draws = jnp.exp(jax.random.uniform(jax.random.fold_in(own, dim), (parts,), jnp.float32, least / len(cuts), high / len(cuts)))
        level = level * jnp.repeat(draws, dims[dim] // parts).reshape([-1 if axis == dim else 1 for axis in range(len(dims))])
    return level


def bell_draw(rng, dims, spread, limit, pieces=(), kind=jnp.bfloat16):
    drawn = jax.random.normal(rng, dims, jnp.float32) * spread
    if len(pieces) > 0:
        drawn = steps_of(rng, dims, pieces, -0.22, 0.18) * drawn
    return jnp.clip(drawn, min=-limit, max=limit).astype(kind)


def setup_inputs(seed: int = 0) -> dict:
    splits = jax.random.split(jax.random.key(seed), 10)
    return {
        "queries": draw_queries(jax.random.fold_in(splits[9], 71), 0),
        "key_tokens": draw_key_tokens(jax.random.fold_in(splits[9], 71), 0),
        "values": bell_draw(splits[2], (SCENES, VIEWS, VROWS, HD), 1.0, 6.0, ((0, 2), (1, 32), (2, 4))),
        "encoder_feats": bell_draw(splits[3], (SCENES, VIEWS, VROWS, E), 1.0, 6.0, ((0, 2), (1, 32), (2, 4))),
        "proj_weight": bell_draw(splits[4], (HD, E), HD ** -0.5, 0.1875, ((0, 32),)),
        "pick_blocks": touch_ends(jax.random.randint(splits[5], (SCENES, VIEWS, N_ROW, PAIRS), 0, QB), jax.random.fold_in(splits[5], 1), 0, QB - 1).astype(jnp.int32),
        "pair_mask": touch_ends((jax.random.randint(splits[6], (SCENES, VIEWS, N_ROW * QB, PAIRS), 0, 4) < 3).astype(jnp.int32), jax.random.fold_in(splits[6], 1), 0, 1),
        "step_ids": touch_ends(jax.random.randint(splits[7], (SCENES, VIEWS), 0, STEPS), jax.random.fold_in(splits[7], 1), 0, STEPS - 1).astype(jnp.int32),
        "step_weight": jnp.clip(jnp.exp(jax.random.uniform(splits[8], (STEPS,), jnp.float32, math.log(2.0), math.log(32.0))), 2.0, 32.0),
    }


def dot_rows(former, latter):
    return lax.dot_general(former, latter, (((1,), (1,)), ((), ())), preferred_element_type=jnp.float32)

def dot_cols(former, latter):
    return lax.dot_general(former, latter, (((0,), (0,)), ((), ())), preferred_element_type=jnp.float32)

def pair_offsets(pair_count):
    half_pairs = pair_count // 2
    return [number + 1 if number < half_pairs else half_pairs - 1 - number for number in range(pair_count)]

def split_heads(matrix):
    return jnp.transpose(matrix.reshape(matrix.shape[0], -1, HS), (1, 0, 2))

def merge_heads(stacked):
    return jnp.transpose(stacked, (1, 0, 2)).reshape(stacked.shape[1], -1)

def allowed_mask(mask_band, band_rows, pair_count):
    own_band = jnp.ones((band_rows, band_rows), dtype=jnp.bool_)
    remote = jnp.repeat(jnp.repeat(mask_band == 1, BLK, axis=0), BLK, axis=1)
    return jnp.concatenate([own_band, remote], axis=1)

def masked_scores(head_query, head_keys, allowed):
    factor = 1.0 / math.sqrt(head_query.shape[1])
    scores = dot_rows(head_query, head_keys) * factor
    return jnp.where(allowed, scores, -jnp.inf)

def head_forward(head_query, head_keys, head_values, allowed):
    scores = masked_scores(head_query, head_keys, allowed)
    largest = lax.optimization_barrier(jnp.max(scores, axis=1, keepdims=True))
    logsum = largest + jnp.log(lax.optimization_barrier(jnp.sum(jnp.exp(scores - largest), axis=1, keepdims=True)))
    attend = jnp.exp(scores - logsum).astype(jnp.bfloat16)
    return (jnp.dot(attend, head_values, preferred_element_type=jnp.float32), logsum)

def head_backward(head_query, head_keys, head_values, allowed, logsum, head_hidden, head_grad):
    factor = 1.0 / math.sqrt(head_query.shape[1])
    scores = masked_scores(head_query, head_keys, allowed)
    attend = jnp.exp(scores - logsum)
    center = lax.optimization_barrier(jnp.sum(head_grad.astype(jnp.float32) * head_hidden.astype(jnp.float32), axis=1, keepdims=True))
    dattend = dot_rows(head_grad, head_values)
    dscores = (attend * (dattend - center)).astype(jnp.bfloat16)
    grad_q = jnp.dot(dscores, head_keys, preferred_element_type=jnp.float32) * factor
    grad_k = dot_cols(dscores, head_query) * factor
    grad_v = dot_cols(attend.astype(jnp.bfloat16), head_grad)
    return (grad_q, grad_k, grad_v)

def attention_forward(band_queries, keys_all, values_all, allowed):

    def one_head(operands):
        return head_forward(operands[0], operands[1], operands[2], allowed)
    head_outputs, logsums = lax.map(one_head, (split_heads(band_queries), split_heads(keys_all), split_heads(values_all)))
    return (merge_heads(head_outputs).astype(jnp.bfloat16), logsums)

def attention_backward(band_queries, keys_all, values_all, allowed, logsums, hidden, grad_hidden):

    def one_head(operands):
        return head_backward(operands[0], operands[1], operands[2], allowed, operands[3], operands[4], operands[5])
    head_grads = lax.map(one_head, (split_heads(band_queries), split_heads(keys_all), split_heads(values_all), logsums, split_heads(hidden), split_heads(grad_hidden)))
    return (merge_heads(head_grads[0]), merge_heads(head_grads[1]), merge_heads(head_grads[2]))

def repa_loss(latent, encoder_band, weight):
    normed = latent * lax.rsqrt(lax.optimization_barrier(jnp.mean(latent * latent, axis=1, keepdims=True)) + 1e-06)
    target = encoder_band.astype(jnp.float32)
    target = target * lax.rsqrt(lax.optimization_barrier(jnp.mean(target * target, axis=1, keepdims=True)) + 1e-06)
    return -weight * jnp.sum(normed * target) / math.sqrt(latent.shape[1])

def reference(queries, key_tokens, values, encoder_feats, proj_weight, pick_blocks, pair_mask, step_ids, step_weight):
    scenes, view_count, view_rows, model_width = queries.shape
    pair_count = pick_blocks.shape[3]
    offsets = pair_offsets(pair_count)
    band_count = view_rows // ROWS_DEV
    blocks = ROWS_DEV // BLK
    total_bands = scenes * view_count * band_count
    zero_index = jnp.zeros((), jnp.int32)

    def band(accumulated, band_index):
        scene_at = band_index // (view_count * band_count)
        view_at = band_index // band_count % view_count
        band_row = band_index % band_count
        row_start = band_row * ROWS_DEV

        def band_slice(source_array, source_view, source_row, length):
            return lax.dynamic_slice(source_array, (scene_at, source_view, source_row, zero_index), (1, 1, length, source_array.shape[3]))[0, 0]
        band_queries = band_slice(queries, view_at, row_start, ROWS_DEV)
        key_parts = [band_slice(key_tokens, view_at, row_start, ROWS_DEV)]
        value_parts = [band_slice(values, view_at, row_start, ROWS_DEV)]
        for number, offset in enumerate(offsets):
            source = (view_at + offset) % view_count
            chosen = pick_blocks[scene_at, source, band_row, number]
            block_start = (row_start + chosen * BLK).astype(jnp.int32)
            key_parts.append(band_slice(key_tokens, source, block_start, BLK))
            value_parts.append(band_slice(values, source, block_start, BLK))
        keys_all = jnp.concatenate(key_parts, axis=0)
        values_all = jnp.concatenate(value_parts, axis=0)
        mask_band = lax.dynamic_slice(pair_mask, (scene_at, view_at, (band_row * blocks).astype(jnp.int32), zero_index), (1, 1, blocks, pair_count))[0, 0]
        allowed = allowed_mask(mask_band, ROWS_DEV, pair_count)
        hidden, logsums = attention_forward(band_queries, keys_all, values_all, allowed)
        latent = jnp.dot(hidden, proj_weight, preferred_element_type=jnp.float32)
        weight = step_weight[step_ids[scene_at, view_at]]
        targets = band_slice(encoder_feats, view_at, row_start, ROWS_DEV)
        grad_latent = jax.grad(repa_loss)(latent, targets, weight).astype(jnp.bfloat16)
        grad_hidden = dot_rows(grad_latent, proj_weight).astype(jnp.bfloat16)
        grad_q, grad_k, grad_v = attention_backward(band_queries, keys_all, values_all, allowed, logsums, hidden, grad_hidden)
        accumulated = accumulated + dot_cols(hidden, grad_latent)
        far_k = grad_k[ROWS_DEV:].astype(jnp.bfloat16).reshape(pair_count, BLK, model_width)
        far_v = grad_v[ROWS_DEV:].astype(jnp.bfloat16).reshape(pair_count, BLK, model_width)
        return (accumulated, (grad_q.astype(jnp.bfloat16), grad_k[:ROWS_DEV], grad_v[:ROWS_DEV], far_k, far_v))
    initial = jnp.zeros((model_width, proj_weight.shape[1]), jnp.float32)
    grad_proj, stacked = lax.scan(band, initial, jnp.arange(total_bands, dtype=jnp.int32))
    block_shape = (scenes, view_count, band_count, blocks, BLK, model_width)

    def assemble(own_terms, far_terms):
        total_sum = own_terms.reshape(block_shape)
        far_terms = far_terms.reshape(scenes, view_count, band_count, pair_count, BLK, model_width)
        for number, offset in enumerate(offsets):
            arriving = jnp.roll(far_terms[:, :, :, number], offset, axis=1).astype(jnp.float32)
            chosen = pick_blocks[:, :, :, number]
            onehot = (chosen[..., None] == jnp.arange(blocks, dtype=jnp.int32)).astype(jnp.float32)
            total_sum = total_sum + onehot[..., None, None] * arriving[:, :, :, None]
        return total_sum.reshape(scenes, view_count, view_rows, model_width).astype(jnp.bfloat16)
    grad_queries = stacked[0].reshape(scenes, view_count, view_rows, model_width)
    grad_keys = assemble(stacked[1], stacked[3])
    grad_values = assemble(stacked[2], stacked[4])
    return (grad_queries, grad_keys, grad_values, grad_proj)
```

```python
import functools
import math

import jax
import jax.numpy as jnp
from jax import lax
from jax.experimental import pallas as pl
from jax.experimental.pallas import tpu as pltpu
from jax.sharding import PartitionSpec as P

HS = 128
BLK = 128
MESH = pl.DeviceIdType.MESH
F32 = jnp.float32
BF16 = jnp.bfloat16
OFFSETS = (1, 2, 3, 4, -1, -2, -3, -4)
ORDER = (4, 3, 5, 2, 6, 1, 7)
SCALE = 1.0 / math.sqrt(HS)
SCALE2 = SCALE * math.log2(math.e)
VMEM = pl.BlockSpec(memory_space=pltpu.VMEM)
ANY = pl.BlockSpec(memory_space=pl.ANY)
LIMIT = 50 * 1024 * 1024


def nt(a, b):
    return lax.dot_general(a, b, (((1,), (1,)), ((), ())), preferred_element_type=F32)


def tn(a, b):
    return lax.dot_general(a, b, (((0,), (0,)), ((), ())), preferred_element_type=F32)


def nn(a, b):
    return jnp.dot(a, b, preferred_element_type=F32)


def place():
    view = lax.axis_index("view")
    return view // 8, view % 8


def at_view(x, z):
    return {"view": x * 8 + z}


def greet(devices):
    barrier = pltpu.get_barrier_semaphore()
    for device in devices:
        pl.semaphore_signal(barrier, inc=1, device_id=device, device_id_type=MESH)
    pl.semaphore_wait(barrier, len(devices))


def z_peers():
    x, z = place()
    return [at_view(x, (z + k) % 8) for k in range(1, 8)]


def x_pair():
    x, z = place()
    return [at_view((x + 1) % 4, z), at_view((x + 3) % 4, z)]


def struct(shape, dtype):
    return jax.ShapeDtypeStruct(shape, dtype)


def remote_params(number):
    return pltpu.CompilerParams(
        collective_id=number, has_side_effects=True, vmem_limit_bytes=LIMIT
    )


def scatter_heads(q, k, v, meta, qh, kh, vh, mh, ss, rs, ls, hs, hr):
    greet(z_peers() + x_pair())
    x, z = place()

    def columns(h):
        return pl.ds(pl.multiple_of(h * HS, HS), HS)

    def pieces(target):
        cols = columns(target)
        return (
            (meta, mh.at[z + 4]),
            (k.at[:, cols], kh.at[z + 4]),
            (v.at[:, cols], vh.at[z + 4]),
            (q.at[:, cols], qh.at[z]),
        )

    local = [
        pltpu.make_async_copy(src, dst, ls.at[n]) for n, (src, dst) in enumerate(pieces(z))
    ]
    sends = {}
    for n in range(4):
        for dist in ORDER:
            target = (z + dist) % 8
            src, dst = pieces(target)[n]
            sends[n, dist] = pltpu.make_async_remote_copy(
                src, dst, ss.at[n, dist], rs.at[n, dist], at_view(x, target), MESH
            )
            sends[n, dist].start()
        local[n].start()
    halo = []
    for dist in (0,) + tuple(reversed(ORDER)):
        origin = (z + 8 - dist) % 8
        for n, buf in enumerate((mh, kh, vh)):
            if dist == 0:
                local[n].wait()
            else:
                sends[n, dist].wait_recv()
            copy = pltpu.make_async_remote_copy(
                buf.at[origin + 4],
                buf.at[(origin + 12) % 16],
                hs.at[n, dist],
                hr.at[n, origin],
                at_view((x + 3 - 2 * (origin // 4)) % 4, z),
                MESH,
            )
            copy.start()
            halo.append(copy)
    local[3].wait()
    for dist in ORDER:
        sends[3, dist].wait_recv()
    for copy in sends.values():
        copy.wait_send()
    for copy in halo:
        copy.wait()


def swap_leading(src, dst, ss, rs, ls):
    greet(z_peers())
    x, z = place()
    copies = []
    for dist in ORDER:
        target = (z + dist) % 8
        copy = pltpu.make_async_remote_copy(
            src.at[target], dst.at[z], ss.at[dist], rs.at[dist], at_view(x, target), MESH
        )
        copy.start()
        copies.append(copy)
    own = pltpu.make_async_copy(src.at[z], dst.at[z], ls)
    own.start()
    own.wait()
    for copy in copies:
        copy.wait()


def picked(ref, meta, chain, m):
    pick = jnp.broadcast_to(meta[chain, m : m + 1, 0:BLK], (BLK, BLK)).astype(BF16)
    return ref[chain, 0:BLK, :] * (1.0 - pick).astype(BF16) + ref[chain, BLK : 2 * BLK, :] * pick


def gather_blocks(i, ref, meta, out):
    out[0 : 2 * BLK, :] = ref[i + 4]
    for m, offset in enumerate(OFFSETS):
        out[(m + 2) * BLK : (m + 3) * BLK, :] = picked(ref, meta, i + 4 + offset, m)


def forward_view(i, qh, kh, vh, mh, probs, inverse, outs, ksel, vsel, scores):
    gather_blocks(i, kh, mh, ksel)
    gather_blocks(i, vh, mh, vsel)
    q = qh[i]
    seen = mh[i + 4][:, BLK:] > 0.5
    largest = None
    for c in range(5):
        rows = slice(c * 256, c * 256 + 256)
        part = nt(ksel[rows, :], q)
        scores[rows, :] = part
        if c == 0:
            largest = jnp.max(part, axis=0, keepdims=True)
        else:
            for b in range(2):
                m = 2 * (c - 1) + b
                top = jnp.max(part[b * BLK : (b + 1) * BLK], axis=0, keepdims=True)
                largest = jnp.maximum(largest, jnp.where(seen[m : m + 1], top, -jnp.inf))
    base = largest * SCALE2
    total = jnp.zeros((1, 256), F32)
    hidden = jnp.zeros((HS, 256), F32)
    for c in range(5):
        halves = []
        for b in range(2):
            rows = slice(c * 256 + b * BLK, c * 256 + (b + 1) * BLK)
            if c == 0:
                shift = base
            else:
                m = 2 * (c - 1) + b
                shift = jnp.where(seen[m : m + 1], base, jnp.inf)
            p = jnp.exp2(scores[rows, :] * SCALE2 - shift)
            total = total + jnp.sum(p, axis=0, keepdims=True)
            p = p.astype(BF16)
            probs[i, rows, :] = p
            halves.append(p)
        rows = slice(c * 256, c * 256 + 256)
        hidden = hidden + tn(vsel[rows, :], jnp.concatenate(halves, axis=0))
    inv = 1.0 / total
    inverse[i] = inv
    outs[i] = (hidden * inv).astype(BF16)


def forward_kernel(qh, kh, vh, mh, probs, inverse, outs, ksel, vsel, scores):
    @pl.loop(0, 8)
    def _(i):
        forward_view(i, qh, kh, vh, mh, probs, inverse, outs, ksel, vsel, scores)


def project(hid, w, feats, weight, grad_hidden, grad_proj):
    h = hid[...].reshape(8 * HS, 256)
    latent = tn(h, w[...])
    width = latent.shape[1]
    target = feats[...].astype(F32)
    target = target * lax.rsqrt(jnp.mean(target * target, axis=1, keepdims=True) + 1e-06)
    grad = target * (-weight / math.sqrt(width))
    r = lax.rsqrt(jnp.mean(latent * latent, axis=1, keepdims=True) + 1e-06)
    along = jnp.mean(grad * latent, axis=1, keepdims=True)
    grad_latent = (r * (grad - latent * (r * r * along))).astype(BF16)
    for head in range(8):
        rows = slice(head * HS, (head + 1) * HS)
        grad_hidden[head] = nt(w[rows, :], grad_latent).astype(BF16)
        grad_proj[rows, :] = nn(hid[head], grad_latent).astype(BF16)


def project_kernel(hid, w, feats, ids, table, grad_hidden, grad_proj):
    project(hid, w, feats, table[ids[0, 0]], grad_hidden, grad_proj)


def spread(acc, meta, chain, m, term):
    pick = jnp.broadcast_to(meta[chain, m : m + 1, 0:BLK], (BLK, BLK))
    upper = term * pick
    acc[chain, 0:BLK, :] += term - upper
    acc[chain, BLK : 2 * BLK, :] += upper


def backward_view(i, qh, kh, vh, mh, probs, inverse, outs, gh, grad_q, acck, accv, ksel, vsel):
    gather_blocks(i, kh, mh, ksel)
    gather_blocks(i, vh, mh, vsel)
    q = qh[i]
    inv = inverse[i]
    g = gh[i]
    gf = g.astype(F32)
    center = jnp.sum(gf * outs[i].astype(F32), axis=0, keepdims=True)
    scaled = (gf * inv).astype(BF16)
    grad_qt = jnp.zeros((HS, 256), F32)
    for c in range(5):
        rows = slice(c * 256, c * 256 + 256)
        p = probs[i, rows, :]
        dp = nn(vsel[rows, :], g)
        ds = (p.astype(F32) * ((dp - center) * inv)).astype(BF16)
        dk = nn(ds, q) * SCALE
        dv = nt(p, scaled)
        grad_qt = grad_qt + tn(ksel[rows, :], ds)
        if c == 0:
            acck[i + 4] += dk
            accv[i + 4] += dv
        else:
            for b in range(2):
                m = 2 * (c - 1) + b
                half = slice(b * BLK, (b + 1) * BLK)
                spread(acck, mh, i + 4 + OFFSETS[m], m, dk[half])
                spread(accv, mh, i + 4 + OFFSETS[m], m, dv[half])
    grad_q[i] = (grad_qt * SCALE).T.astype(BF16)


def backward_kernel(
    qh, kh, vh, mh, probs, inverse, outs, gh, grad_q, ownk, ownv, edgek, edgev, acck, accv, ksel, vsel
):
    acck[...] = jnp.zeros_like(acck)
    accv[...] = jnp.zeros_like(accv)

    @pl.loop(0, 8)
    def _(i):
        backward_view(
            i, qh, kh, vh, mh, probs, inverse, outs, gh, grad_q, acck, accv, ksel, vsel
        )

    for acc, own, edge in ((acck, ownk, edgek), (accv, ownv, edgev)):
        own[...] = acc[4:12]
        edge[0:4] = acc[12:16].astype(BF16)
        edge[4:8] = acc[0:4].astype(BF16)


def return_heads(
    grad_q, ownk, ownv, edgek, edgev, oq, ok, ov, landk, landv, fullk, fullv, ss, rs, ls, hs, hr
):
    greet(z_peers() + x_pair())
    x, z = place()
    cols = pl.ds(pl.multiple_of(z * HS, HS), HS)

    def send(n, src, dst, dist):
        target = (z + dist) % 8
        copy = pltpu.make_async_remote_copy(
            src.at[target], dst.at[:, cols], ss.at[n, dist], rs.at[n, dist], at_view(x, target), MESH
        )
        copy.start()
        return copy

    halo = {}
    for dist in ORDER + (0,):
        view = (z + dist) % 8
        for n, (src, dst) in enumerate(((edgek, landk), (edgev, landv))):
            copy = pltpu.make_async_remote_copy(
                src.at[view],
                dst.at[view],
                hs.at[n, dist],
                hr.at[n, dist],
                at_view((x + 1 + 2 * (view // 4)) % 4, z),
                MESH,
            )
            copy.start()
            halo[n, dist] = copy
    copies = [send(0, grad_q, oq, dist) for dist in ORDER]
    local = [pltpu.make_async_copy(grad_q.at[z], oq.at[:, cols], ls.at[0])]
    local[0].start()
    for dist in ORDER + (0,):
        view = (z + dist) % 8
        for n, (own, land, full, dst) in enumerate(
            ((ownk, landk, fullk, ok), (ownv, landv, fullv, ov))
        ):
            halo[n, dist].wait_recv()
            full[view] = (own[view] + land[view].astype(F32)).astype(BF16)
            if dist:
                copies.append(send(n + 1, full, dst, dist))
            else:
                copy = pltpu.make_async_copy(full.at[z], dst.at[:, cols], ls.at[n + 1])
                copy.start()
                local.append(copy)
    for copy in local + copies:
        copy.wait()
    for copy in halo.values():
        copy.wait_send()


def total_of(parts):
    total = parts[0].astype(F32)
    for part in parts[1:]:
        total = total + part.astype(F32)
    return total


def reduce_projector(g, out, c1, a, c2, b, c3, c, c4, d, ss, rs):
    x, z = place()
    y = lax.axis_index("row")
    core = lax.axis_index("dp")
    other = {"dp": 1 - core}
    ys = [(y + k) % 4 for k in range(1, 4)]
    xs = [(x + k) % 4 for k in range(1, 4)]
    root = 2 * y + core
    final = [(dy, dc) for dy in range(4) for dc in range(2) if (dy, dc) != (0, 0)]
    all_final = [{"row": (y + dy) % 4, "dp": (core + dc) % 2} for dy, dc in final]
    greet(all_final + [at_view(v, z) for v in xs] + z_peers())

    def copy(src, dst, n, device):
        return pltpu.make_async_remote_copy(src, dst, ss.at[n], rs.at[n], device, MESH)

    first = copy(g.at[:, :, 1 - core], c1, 0, other)
    first.start()
    first.wait()
    for i in range(4):
        for j in range(4):
            a[i, j] = total_of([g[i, j, core], c1[i, j]]).astype(BF16)
    sends = []
    for n, k in enumerate(ys):
        sends.append(copy(a.at[:, k], c2.at[n], 1 + n, {"row": k}))
        sends[-1].start()
    for s in sends:
        s.wait()
    b[...] = total_of([a[:, y], c2[0], c2[1], c2[2]]).astype(BF16)
    sends = []
    for n, k in enumerate(xs):
        sends.append(copy(b.at[k], c3.at[n], 4 + n, at_view(k, z)))
        sends[-1].start()
    for s in sends:
        s.wait()
    c[...] = total_of([b[x], c3[0], c3[1], c3[2]]).astype(BF16)
    is_root = z == root

    @pl.when(jnp.logical_not(is_root))
    def _():
        up = pltpu.make_async_remote_copy(
            c, c4.at[z], ss.at[7], rs.at[8 + z], at_view(x, root), MESH
        )
        up.start()
        up.wait_send()

    @pl.when(is_root)
    def _():
        c4[z] = c[...]
        for k in range(1, 8):
            origin = (z + k) % 8
            pltpu.make_async_remote_copy(
                c, c4.at[origin], ss.at[7], rs.at[8 + origin], at_view(x, origin), MESH
            ).wait_recv()
        d[...] = total_of([c4[k] for k in range(8)]).astype(BF16)
        down = []
        for n, device in enumerate(all_final):
            down.append(
                pltpu.make_async_remote_copy(d, d, ss.at[16 + n], rs.at[7], device, MESH)
            )
            down[-1].start()
        for s in down:
            s.wait_send()

    @pl.when(jnp.logical_not(is_root))
    def _():
        pltpu.make_async_remote_copy(d, d, ss.at[16], rs.at[7], other, MESH).wait_recv()

    out[...] = d[...].astype(F32)


def local(
    queries,
    key_tokens,
    values,
    encoder_feats,
    proj_weight,
    pick_blocks,
    pair_mask,
    step_ids,
    step_weight,
):
    dma = pltpu.SemaphoreType.DMA
    rows, width = queries.shape[2:]
    features = encoder_feats.shape[3]
    weights = lax.all_gather(proj_weight, "view", axis=0, tiled=True)
    flags = jnp.concatenate([pick_blocks[0, 0], pair_mask[0, 0]], axis=0).astype(F32)
    meta = jnp.broadcast_to(flags.T[:, :, None], (8, 3, BLK)).reshape(8, 3 * BLK)
    qh, kh, vh, mh = pl.pallas_call(
        scatter_heads,
        out_shape=[
            struct((8, rows, HS), BF16),
            struct((16, rows, HS), BF16),
            struct((16, rows, HS), BF16),
            struct((16, 8, 3 * BLK), F32),
        ],
        in_specs=[ANY] * 4,
        out_specs=[ANY] * 4,
        scratch_shapes=[dma((4, 8)), dma((4, 8)), dma((4,)), dma((3, 8)), dma((3, 8))],
        compiler_params=remote_params(1),
        name="scatter_heads",
    )(queries[0, 0], key_tokens[0, 0], values[0, 0], meta)
    probs, inverse, outs = pl.pallas_call(
        forward_kernel,
        out_shape=[
            struct((8, 5 * 256, rows), BF16),
            struct((8, 1, rows), F32),
            struct((8, HS, rows), BF16),
        ],
        in_specs=[VMEM] * 4,
        out_specs=[VMEM] * 3,
        scratch_shapes=[
            pltpu.VMEM((5 * 256, HS), BF16),
            pltpu.VMEM((5 * 256, HS), BF16),
            pltpu.VMEM((5 * 256, rows), F32),
        ],
        compiler_params=pltpu.CompilerParams(vmem_limit_bytes=LIMIT),
        name="forward",
    )(qh, kh, vh, mh)

    def swap(array, number, name):
        return pl.pallas_call(
            swap_leading,
            out_shape=struct(array.shape, array.dtype),
            in_specs=[ANY],
            out_specs=ANY,
            scratch_shapes=[dma((8,)), dma((8,)), dma(())],
            compiler_params=remote_params(number),
            name=name,
        )(array)

    hidden = swap(outs, 2, "swap_hidden")
    grad_hidden, grad_proj = pl.pallas_call(
        project_kernel,
        out_shape=[struct((8, HS, rows), BF16), struct((width, features), BF16)],
        in_specs=[VMEM, VMEM, VMEM]
        + [pl.BlockSpec(memory_space=pltpu.SMEM)] * 2,
        out_specs=[VMEM] * 2,
        compiler_params=pltpu.CompilerParams(vmem_limit_bytes=LIMIT),
        name="project",
    )(hidden, weights, encoder_feats[0, 0], step_ids, step_weight)
    gh = swap(grad_hidden, 3, "swap_grad")
    shard = (width // 32, features)
    grad_rows = pl.pallas_call(
        reduce_projector,
        out_shape=struct(shard, F32),
        in_specs=[VMEM],
        out_specs=VMEM,
        scratch_shapes=[
            pltpu.VMEM((4, 4) + shard, BF16),
            pltpu.VMEM((4, 4) + shard, BF16),
            pltpu.VMEM((3, 4) + shard, BF16),
            pltpu.VMEM((4,) + shard, BF16),
            pltpu.VMEM((3,) + shard, BF16),
            pltpu.VMEM(shard, BF16),
            pltpu.VMEM((8,) + shard, BF16),
            pltpu.VMEM(shard, BF16),
            dma((24,)),
            dma((24,)),
        ],
        compiler_params=remote_params(4),
        name="reduce_projector",
    )(grad_proj.reshape((4, 4, 2) + shard))
    head = struct((8, rows, HS), BF16)
    wide = struct((8, rows, HS), F32)
    grad_q, ownk, ownv, edgek, edgev = pl.pallas_call(
        backward_kernel,
        out_shape=[head, wide, wide, head, head],
        in_specs=[VMEM] * 8,
        out_specs=[VMEM] * 5,
        scratch_shapes=[
            pltpu.VMEM((16, rows, HS), F32),
            pltpu.VMEM((16, rows, HS), F32),
            pltpu.VMEM((5 * 256, HS), BF16),
            pltpu.VMEM((5 * 256, HS), BF16),
        ],
        compiler_params=pltpu.CompilerParams(vmem_limit_bytes=LIMIT),
        name="backward",
    )(qh, kh, vh, mh, probs, inverse, outs, gh)
    whole = struct((rows, width), BF16)
    gq, gk, gv = pl.pallas_call(
        return_heads,
        out_shape=[whole] * 3,
        in_specs=[VMEM] * 5,
        out_specs=[VMEM] * 3,
        scratch_shapes=[pltpu.VMEM((8, rows, HS), BF16)] * 4
        + [dma((3, 8)), dma((3, 8)), dma((3,)), dma((2, 8)), dma((2, 8))],
        compiler_params=remote_params(5),
        name="return_heads",
    )(grad_q, ownk, ownv, edgek, edgev)
    return gq[None, None], gk[None, None], gv[None, None], grad_rows


def solution(mesh):
    band = P("dp", "view", "row", None)
    return jax.shard_map(
        local,
        mesh=mesh,
        in_specs=(
            band,
            band,
            band,
            band,
            P("view", None),
            band,
            band,
            P("dp", "view"),
            P(),
        ),
        out_specs=(band, band, band, P("view", None)),
        check_vma=False,
    )
```

```python
import functools
import math

import jax
import jax.numpy as jnp
from jax import lax
from jax.experimental import pallas as pl
from jax.experimental.pallas import tpu as pltpu
from jax.sharding import PartitionSpec as P

HS = 128
BLK = 128
MESH = pl.DeviceIdType.MESH
F32 = jnp.float32
BF16 = jnp.bfloat16
OFFSETS = (1, 2, 3, 4, -1, -2, -3, -4)
ORDER = (4, 3, 5, 2, 6, 1, 7)
NEAR = (1, 7, 2, 6, 3, 5, 4)
SCALE = 1.0 / math.sqrt(HS)
SCALE2 = SCALE * math.log2(math.e)
VMEM = pl.BlockSpec(memory_space=pltpu.VMEM)
ANY = pl.BlockSpec(memory_space=pl.ANY)
LIMIT = 60 * 1024 * 1024


def nt(a, b):
    return lax.dot_general(a, b, (((1,), (1,)), ((), ())), preferred_element_type=F32)


def tn(a, b):
    return lax.dot_general(a, b, (((0,), (0,)), ((), ())), preferred_element_type=F32)


def nn(a, b):
    return jnp.dot(a, b, preferred_element_type=F32)


def place():
    view = lax.axis_index("view")
    return view // 8, view % 8


def at_view(x, z):
    return {"view": x * 8 + z}


def greet(devices):
    barrier = pltpu.get_barrier_semaphore()
    for device in devices:
        pl.semaphore_signal(barrier, inc=1, device_id=device, device_id_type=MESH)
    pl.semaphore_wait(barrier, len(devices))


def z_peers():
    x, z = place()
    return [at_view(x, (z + k) % 8) for k in range(1, 8)]


def x_pair():
    x, z = place()
    return [at_view((x + 1) % 4, z), at_view((x + 3) % 4, z)]


def struct(shape, dtype):
    return jax.ShapeDtypeStruct(shape, dtype)


def remote_params(number):
    return pltpu.CompilerParams(
        collective_id=number, has_side_effects=True, vmem_limit_bytes=LIMIT
    )


def picked(ref, meta, chain, m):
    pick = jnp.broadcast_to(meta[chain, m : m + 1, 0:BLK], (BLK, BLK)).astype(BF16)
    return ref[chain, 0:BLK, :] * (1.0 - pick).astype(BF16) + ref[chain, BLK : 2 * BLK, :] * pick


def gather_blocks(i, ref, meta, out):
    out[0 : 2 * BLK, :] = ref[i + 4]
    for m, offset in enumerate(OFFSETS):
        out[(m + 2) * BLK : (m + 3) * BLK, :] = picked(ref, meta, i + 4 + offset, m)


def forward_view(i, qh, kh, vh, mh, probs, inverse, outs, ksel, vsel, scores):
    gather_blocks(i, kh, mh, ksel)
    gather_blocks(i, vh, mh, vsel)
    q = qh[i]
    seen = mh[i + 4][:, BLK:] > 0.5
    largest = None
    for c in range(5):
        rows = slice(c * 256, c * 256 + 256)
        part = nt(ksel[rows, :], q)
        scores[rows, :] = part
        if c == 0:
            largest = jnp.max(part, axis=0, keepdims=True)
        else:
            for b in range(2):
                m = 2 * (c - 1) + b
                top = jnp.max(part[b * BLK : (b + 1) * BLK], axis=0, keepdims=True)
                largest = jnp.maximum(largest, jnp.where(seen[m : m + 1], top, -jnp.inf))
    base = largest * SCALE2
    total = jnp.zeros((1, 256), F32)
    hidden = jnp.zeros((HS, 256), F32)
    for c in range(5):
        halves = []
        for b in range(2):
            rows = slice(c * 256 + b * BLK, c * 256 + (b + 1) * BLK)
            if c == 0:
                shift = base
            else:
                m = 2 * (c - 1) + b
                shift = jnp.where(seen[m : m + 1], base, jnp.inf)
            p = jnp.exp2(scores[rows, :] * SCALE2 - shift)
            total = total + jnp.sum(p, axis=0, keepdims=True)
            p = p.astype(BF16)
            probs[i, rows, :] = p
            halves.append(p)
        rows = slice(c * 256, c * 256 + 256)
        hidden = hidden + tn(vsel[rows, :], jnp.concatenate(halves, axis=0))
    inv = 1.0 / total
    inverse[i] = inv
    outs[i] = (hidden * inv).astype(BF16)


def project(hid, w, feats, weight, grad_hidden, grad_proj):
    features = feats.shape[1]
    latent = tn(hid[...].reshape(8 * HS, 256), w[...].reshape(8 * HS, features))
    target = feats[...].astype(F32)
    target = target * lax.rsqrt(jnp.mean(target * target, axis=1, keepdims=True) + 1e-06)
    grad = target * (-weight / math.sqrt(features))
    r = lax.rsqrt(jnp.mean(latent * latent, axis=1, keepdims=True) + 1e-06)
    along = jnp.mean(grad * latent, axis=1, keepdims=True)
    grad_latent = (r * (grad - latent * (r * r * along))).astype(BF16)
    for head in range(8):
        part = w[head // 2, 2 * (head % 2) : 2 * (head % 2) + 2].reshape(HS, features)
        grad_hidden[head] = nt(part, grad_latent).astype(BF16)
        grad_proj[head // 2, 2 * (head % 2) : 2 * (head % 2) + 2] = (
            nn(hid[head], grad_latent).astype(BF16).reshape(2, 2, HS // 4, features)
        )


def spread(acc, meta, chain, m, term):
    pick = jnp.broadcast_to(meta[chain, m : m + 1, 0:BLK], (BLK, BLK))
    upper = term * pick
    acc[chain, 0:BLK, :] += term - upper
    acc[chain, BLK : 2 * BLK, :] += upper


def backward_view(i, qh, kh, vh, mh, probs, inverse, outs, gh, grad_q, acck, accv, ksel, vsel):
    gather_blocks(i, kh, mh, ksel)
    gather_blocks(i, vh, mh, vsel)
    q = qh[i]
    inv = inverse[i]
    g = gh[i]
    gf = g.astype(F32)
    center = jnp.sum(gf * outs[i].astype(F32), axis=0, keepdims=True)
    scaled = (gf * inv).astype(BF16)
    grad_qt = jnp.zeros((HS, 256), F32)
    for c in range(5):
        rows = slice(c * 256, c * 256 + 256)
        p = probs[i, rows, :]
        dp = nn(vsel[rows, :], g)
        ds = (p.astype(F32) * ((dp - center) * inv)).astype(BF16)
        dk = nn(ds, q) * SCALE
        dv = nt(p, scaled)
        grad_qt = grad_qt + tn(ksel[rows, :], ds)
        if c == 0:
            acck[i + 4] += dk
            accv[i + 4] += dv
        else:
            for b in range(2):
                m = 2 * (c - 1) + b
                half = slice(b * BLK, (b + 1) * BLK)
                spread(acck, mh, i + 4 + OFFSETS[m], m, dk[half])
                spread(accv, mh, i + 4 + OFFSETS[m], m, dv[half])
    grad_q[i] = (grad_qt * SCALE).T.astype(BF16)


def total_of(parts):
    total = parts[0].astype(F32)
    for part in parts[1:]:
        total = total + part.astype(F32)
    return total


def nearest(k):
    odd = k % 2
    return (odd * ((k + 1) // 2) + (1 - odd) * (8 - k // 2)) % 8


def whole_kernel(
    q,
    k,
    v,
    meta,
    wshard,
    feats,
    ids,
    table,
    oq,
    ok,
    ov,
    grad_rows,
    qh,
    kh,
    vh,
    mh,
    w,
    probs,
    inverse,
    outs,
    hid,
    grad_hidden,
    gh,
    g,
    c1,
    a,
    c2,
    b,
    c3,
    c,
    c4,
    d,
    grad_q,
    acck,
    accv,
    edgek,
    edgev,
    landk,
    landv,
    fullk,
    fullv,
    ksel,
    vsel,
    scores,
    ls,
    ss,
    rs,
    hs,
    hr,
    ws,
    wr,
    os,
    ors,
    gs,
    gr,
    ps,
    pr,
    qs,
    qr,
    es,
    er,
    fs,
    fr,
):
    x, z = place()
    y = lax.axis_index("row")
    core = lax.axis_index("dp")
    root = 2 * y + core
    is_root = z == root
    other = {"dp": 1 - core}
    xs = [(x + n) % 4 for n in range(1, 4)]
    ys = [(y + n) % 4 for n in range(1, 4)]
    turns = [(dy, dc) for dy in range(4) for dc in range(2) if (dy, dc) != (0, 0)]
    column = [{"row": (y + dy) % 4, "dp": (core + dc) % 2} for dy, dc in turns]
    greet(z_peers() + [at_view(n, z) for n in xs] + column)

    def remote(src, dst, send_sem, recv_sem, device):
        return pltpu.make_async_remote_copy(src, dst, send_sem, recv_sem, device, MESH)

    def columns(h):
        return pl.ds(pl.multiple_of(h * HS, HS), HS)

    def pieces(target, n):
        cols = columns(target)
        return (
            (meta, mh.at[z + 4]),
            (k.at[:, cols], kh.at[z + 4]),
            (v.at[:, cols], vh.at[z + 4]),
            (q.at[:, cols], qh.at[z]),
        )[n]

    def scatter(n, dist):
        target = (z + dist) % 8
        src, dst = pieces(target, n)
        return remote(src, dst, ss.at[n, dist], rs.at[n, dist], at_view(x, target))

    def halo(n, dist):
        origin = (z + 8 - dist) % 8
        buf = (mh, kh, vh)[n]
        return remote(
            buf.at[origin + 4],
            buf.at[(origin + 12) % 16],
            hs.at[n, dist],
            hr.at[n, origin],
            at_view((x + 3 - 2 * (origin // 4)) % 4, z),
        )

    own = [pltpu.make_async_copy(*pieces(z, n), ls.at[n]) for n in range(4)]
    for n in range(4):
        for dist in ORDER if n < 3 else NEAR:
            scatter(n, dist).start()
        own[n].start()
    mine = w.at[x, y, core]

    @pl.when(is_root)
    def _():
        copy = pltpu.make_async_copy(wshard, mine, ls.at[4])
        copy.start()
        copy.wait()
        sends = [
            remote(mine, mine, ws.at[n], wr.at[0], at_view(x, (z + n + 1) % 8)) for n in range(7)
        ]
        for s in sends:
            s.start()
        for s in sends:
            s.wait_send()

    @pl.when(jnp.logical_not(is_root))
    def _():
        remote(mine, mine, ws.at[0], wr.at[0], other).wait_recv()

    along_x = [
        remote(mine, mine, ws.at[7 + n], wr.at[1 + n], at_view(t, z)) for n, t in enumerate(xs)
    ]
    for s in along_x:
        s.start()
    for n in range(3):
        own[n].wait()
        halo(n, 0).start()
    for s in along_x:
        s.wait()
    mine_y = w.at[:, y, core]
    along_y = [
        remote(mine_y, mine_y, ws.at[10 + n], wr.at[4 + n], {"row": t}) for n, t in enumerate(ys)
    ]
    for s in along_y:
        s.start()

    for n in range(3):

        @pl.loop(1, 8)
        def _(turn):
            dist = nearest(turn)
            scatter(n, dist).wait_recv()
            halo(n, dist).start()

    for s in along_y:
        s.wait()
    mine_c = w.at[:, :, core]
    along_c = remote(mine_c, mine_c, ws.at[13], wr.at[7], other)
    along_c.start()

    @pl.loop(0, 8)
    def _(dist):
        for n in range(3):
            halo(n, dist).wait()

    def give_hidden(dist):
        target = (z + 8 - dist) % 8
        return remote(
            outs.at[target], hid.at[z], os.at[dist], ors.at[dist], at_view(x, target)
        )

    own[3].wait()

    @pl.loop(0, 8)
    def _(turn):
        dist = nearest(turn)
        view = (z + 8 - dist) % 8

        @pl.when(turn > 0)
        def _():
            scatter(3, dist).wait_recv()

        forward_view(view, qh, kh, vh, mh, probs, inverse, outs, ksel, vsel, scores)

        @pl.when(turn > 0)
        def _():
            give_hidden(dist).start()

    hid[z] = outs[z]

    @pl.loop(1, 8)
    def _(dist):
        for n in range(4):
            scatter(n, dist).wait_send()
        give_hidden(dist).wait()

    along_c.wait()
    project(hid, w, feats, table[ids[0, 0]], grad_hidden, g)

    def give_grad(dist):
        target = (z + dist) % 8
        return remote(
            grad_hidden.at[target], gh.at[z], gs.at[dist], gr.at[dist], at_view(x, target)
        )

    for dist in NEAR:
        give_grad(dist).start()
    gh[z] = grad_hidden[z]
    acck[...] = jnp.zeros_like(acck)
    accv[...] = jnp.zeros_like(accv)
    across = remote(g.at[:, :, 1 - core], c1, ps.at[0], pr.at[0], other)
    across.start()
    reduce_y = [
        remote(a.at[:, t], c2.at[n], ps.at[1 + n], pr.at[1 + n], {"row": t})
        for n, t in enumerate(ys)
    ]
    reduce_x = [
        remote(b.at[t], c3.at[n], ps.at[4 + n], pr.at[4 + n], at_view(t, z))
        for n, t in enumerate(xs)
    ]
    reduce_z = remote(c, c4.at[z], ps.at[7], pr.at[8 + z], at_view(x, root))
    down = [remote(d, d, ps.at[8 + n], pr.at[7], device) for n, device in enumerate(column)]

    def give_q(dist):
        target = (z + 8 - dist) % 8
        return remote(
            grad_q.at[target], oq.at[:, columns(z)], qs.at[dist], qr.at[dist], at_view(x, target)
        )

    @pl.loop(0, 8)
    def _(turn):
        dist = nearest(turn)
        view = (z + 8 - dist) % 8

        @pl.when(turn > 0)
        def _():
            give_grad(dist).wait_recv()

        backward_view(
            view, qh, kh, vh, mh, probs, inverse, outs, gh, grad_q, acck, accv, ksel, vsel
        )

        @pl.when(turn > 0)
        def _():
            give_q(dist).start()

        @pl.when(turn == 1)
        def _():
            across.wait()
            for i in range(4):
                for j in range(4):
                    a[i, j] = total_of([g[i, j, core], c1[i, j]]).astype(BF16)
            for s in reduce_y:
                s.start()

        @pl.when(turn == 5)
        def _():
            for s in reduce_y:
                s.wait()
            b[...] = total_of([a[:, y], c2[0], c2[1], c2[2]]).astype(BF16)
            for s in reduce_x:
                s.start()

        @pl.when(turn == 7)
        def _():
            for s in reduce_x:
                s.wait()
            c[...] = total_of([b[x], c3[0], c3[1], c3[2]]).astype(BF16)

            @pl.when(jnp.logical_not(is_root))
            def _():
                reduce_z.start()

    own_q = pltpu.make_async_copy(grad_q.at[z], oq.at[:, columns(z)], ls.at[0])
    own_q.start()

    def edge(n, dist):
        view = (z + dist) % 8
        src, dst = ((edgek, landk), (edgev, landv))[n]
        return remote(
            src.at[view],
            dst.at[view],
            es.at[n, dist],
            er.at[n, dist],
            at_view((x + 1 + 2 * (view // 4)) % 4, z),
        )

    def give_terms(n, dist):
        target = (z + dist) % 8
        src, dst = ((fullk, ok), (fullv, ov))[n]
        return remote(
            src.at[target], dst.at[:, columns(z)], fs.at[n, dist], fr.at[n, dist], at_view(x, target)
        )

    @pl.loop(1, 9)
    def _(turn):
        dist = nearest(turn % 8)
        view = (z + dist) % 8
        for n, (acc, buf) in enumerate(((acck, edgek), (accv, edgev))):
            buf[view] = acc[(view + 12) % 16].astype(BF16)
            edge(n, dist).start()

    @pl.loop(1, 9)
    def _(turn):
        dist = nearest(turn % 8)
        view = (z + dist) % 8
        for n, (acc, land, full) in enumerate(((acck, landk, fullk), (accv, landv, fullv))):
            edge(n, dist).wait_recv()
            full[view] = (acc[view + 4] + land[view].astype(F32)).astype(BF16)

            @pl.when(turn < 8)
            def _():
                give_terms(n, dist).start()

    own_k = pltpu.make_async_copy(fullk.at[z], ok.at[:, columns(z)], ls.at[1])
    own_v = pltpu.make_async_copy(fullv.at[z], ov.at[:, columns(z)], ls.at[2])
    own_k.start()
    own_v.start()

    @pl.when(jnp.logical_not(is_root))
    def _():
        reduce_z.wait_send()
        down[0].wait_recv()

    @pl.when(is_root)
    def _():
        c4[z] = c[...]
        for n in range(1, 8):
            origin = (z + n) % 8
            remote(c, c4.at[origin], ps.at[7], pr.at[8 + origin], at_view(x, origin)).wait_recv()
        d[...] = total_of([c4[n] for n in range(8)]).astype(BF16)
        for s in down:
            s.start()
        for s in down:
            s.wait_send()

    grad_rows[...] = d[...].astype(F32)

    @pl.loop(1, 8)
    def _(dist):
        give_grad(dist).wait_send()
        give_q(dist).wait()
        for n in range(2):
            give_terms(n, dist).wait()

    @pl.loop(0, 8)
    def _(dist):
        for n in range(2):
            edge(n, dist).wait_send()

    own_q.wait()
    own_k.wait()
    own_v.wait()


def local(
    queries,
    key_tokens,
    values,
    encoder_feats,
    proj_weight,
    pick_blocks,
    pair_mask,
    step_ids,
    step_weight,
):
    dma = pltpu.SemaphoreType.DMA
    rows, width = queries.shape[2:]
    features = encoder_feats.shape[3]
    keys = 5 * 256
    shard = (width // 32, features)
    flags = jnp.concatenate([pick_blocks[0, 0], pair_mask[0, 0]], axis=0).astype(F32)
    meta = jnp.broadcast_to(flags.T[:, :, None], (8, 3, BLK)).reshape(8, 3 * BLK)
    smem = pl.BlockSpec(memory_space=pltpu.SMEM)
    whole = struct((rows, width), BF16)
    head = pltpu.VMEM((8, rows, HS), BF16)
    chain = pltpu.VMEM((16, rows, HS), BF16)
    turned = pltpu.VMEM((8, HS, rows), BF16)
    gq, gk, gv, grad_rows = pl.pallas_call(
        whole_kernel,
        out_shape=[whole, whole, whole, struct(shard, F32)],
        in_specs=[ANY] * 5 + [VMEM] + [smem] * 2,
        out_specs=[ANY] * 3 + [VMEM],
        scratch_shapes=[
            head,
            chain,
            chain,
            pltpu.VMEM((16, 8, 3 * BLK), F32),
            pltpu.VMEM((4, 4, 2) + shard, BF16),
            pltpu.VMEM((8, keys, rows), BF16),
            pltpu.VMEM((8, 1, rows), F32),
            turned,
            turned,
            turned,
            turned,
            pltpu.VMEM((4, 4, 2) + shard, BF16),
            pltpu.VMEM((4, 4) + shard, BF16),
            pltpu.VMEM((4, 4) + shard, BF16),
            pltpu.VMEM((3, 4) + shard, BF16),
            pltpu.VMEM((4,) + shard, BF16),
            pltpu.VMEM((3,) + shard, BF16),
            pltpu.VMEM(shard, BF16),
            pltpu.VMEM((8,) + shard, BF16),
            pltpu.VMEM(shard, BF16),
            head,
            pltpu.VMEM((16, rows, HS), F32),
            pltpu.VMEM((16, rows, HS), F32),
            head,
            head,
            head,
            head,
            head,
            head,
            pltpu.VMEM((keys, HS), BF16),
            pltpu.VMEM((keys, HS), BF16),
            pltpu.VMEM((keys, rows), F32),
            dma((5,)),
            dma((4, 8)),
            dma((4, 8)),
            dma((3, 8)),
            dma((3, 8)),
            dma((14,)),
            dma((8,)),
            dma((8,)),
            dma((8,)),
            dma((8,)),
            dma((8,)),
            dma((16,)),
            dma((16,)),
            dma((8,)),
            dma((8,)),
            dma((2, 8)),
            dma((2, 8)),
            dma((2, 8)),
            dma((2, 8)),
        ],
        compiler_params=remote_params(1),
        name="whole",
    )(
        queries[0, 0],
        key_tokens[0, 0],
        values[0, 0],
        meta,
        proj_weight,
        encoder_feats[0, 0],
        step_ids,
        step_weight,
    )
    return gq[None, None], gk[None, None], gv[None, None], grad_rows


def solution(mesh):
    band = P("dp", "view", "row", None)
    return jax.shard_map(
        local,
        mesh=mesh,
        in_specs=(
            band,
            band,
            band,
            band,
            P("view", None),
            band,
            band,
            P("dp", "view"),
            P(),
        ),
        out_specs=(band, band, band, P("view", None)),
        check_vma=False,
    )
```

```python
import functools
import math

import jax
import jax.numpy as jnp
from jax import lax
from jax.experimental import pallas as pl
from jax.experimental.pallas import tpu as pltpu
from jax.sharding import PartitionSpec as P

HS = 128
BLK = 128
MESH = pl.DeviceIdType.MESH
F32 = jnp.float32
BF16 = jnp.bfloat16
OFFSETS = (1, 2, 3, 4, -1, -2, -3, -4)
ORDER = (4, 3, 5, 2, 6, 1, 7)
NEAR = (1, 7, 2, 6, 3, 5, 4)
SCALE = 1.0 / math.sqrt(HS)
SCALE2 = SCALE * math.log2(math.e)
VMEM = pl.BlockSpec(memory_space=pltpu.VMEM)
ANY = pl.BlockSpec(memory_space=pl.ANY)
LIMIT = 60 * 1024 * 1024


def nt(a, b):
    return lax.dot_general(a, b, (((1,), (1,)), ((), ())), preferred_element_type=F32)


def tn(a, b):
    return lax.dot_general(a, b, (((0,), (0,)), ((), ())), preferred_element_type=F32)


def nn(a, b):
    return jnp.dot(a, b, preferred_element_type=F32)


def place():
    view = lax.axis_index("view")
    return view // 8, view % 8


def at_view(x, z):
    return {"view": x * 8 + z}


def greet(devices):
    barrier = pltpu.get_barrier_semaphore()
    for device in devices:
        pl.semaphore_signal(barrier, inc=1, device_id=device, device_id_type=MESH)
    pl.semaphore_wait(barrier, len(devices))


def z_peers():
    x, z = place()
    return [at_view(x, (z + k) % 8) for k in range(1, 8)]


def x_pair():
    x, z = place()
    return [at_view((x + 1) % 4, z), at_view((x + 3) % 4, z)]


def struct(shape, dtype):
    return jax.ShapeDtypeStruct(shape, dtype)


def remote_params(number):
    return pltpu.CompilerParams(
        collective_id=number, has_side_effects=True, vmem_limit_bytes=LIMIT
    )


def picked(ref, meta, chain, m):
    pick = jnp.broadcast_to(meta[chain, m : m + 1, 0:BLK], (BLK, BLK)).astype(BF16)
    return ref[chain, 0:BLK, :] * (1.0 - pick).astype(BF16) + ref[chain, BLK : 2 * BLK, :] * pick


def gather_blocks(i, ref, meta, out):
    out[0 : 2 * BLK, :] = ref[i + 4]
    for m, offset in enumerate(OFFSETS):
        out[(m + 2) * BLK : (m + 3) * BLK, :] = picked(ref, meta, i + 4 + offset, m)


def forward_view(i, qh, kh, vh, mh, probs, inverse, outs, ksel, vsel, scores):
    gather_blocks(i, kh, mh, ksel)
    gather_blocks(i, vh, mh, vsel)
    q = qh[i]
    seen = mh[i + 4][:, BLK:] > 0.5
    largest = None
    for c in range(5):
        rows = slice(c * 256, c * 256 + 256)
        part = nt(ksel[rows, :], q)
        scores[rows, :] = part
        if c == 0:
            largest = jnp.max(part, axis=0, keepdims=True)
        else:
            for b in range(2):
                m = 2 * (c - 1) + b
                top = jnp.max(part[b * BLK : (b + 1) * BLK], axis=0, keepdims=True)
                largest = jnp.maximum(largest, jnp.where(seen[m : m + 1], top, -jnp.inf))
    base = largest * SCALE2
    total = jnp.zeros((1, 256), F32)
    hidden = jnp.zeros((HS, 256), F32)
    for c in range(5):
        halves = []
        for b in range(2):
            rows = slice(c * 256 + b * BLK, c * 256 + (b + 1) * BLK)
            if c == 0:
                shift = base
            else:
                m = 2 * (c - 1) + b
                shift = jnp.where(seen[m : m + 1], base, jnp.inf)
            p = jnp.exp2(scores[rows, :] * SCALE2 - shift)
            total = total + jnp.sum(p, axis=0, keepdims=True)
            p = p.astype(BF16)
            probs[i, rows, :] = p
            halves.append(p)
        rows = slice(c * 256, c * 256 + 256)
        hidden = hidden + tn(vsel[rows, :], jnp.concatenate(halves, axis=0))
    inv = 1.0 / total
    inverse[i] = inv
    outs[i] = (hidden * inv).astype(BF16)


def project(hid, w, feats, weight, grad_hidden, grad_proj):
    features = feats.shape[1]
    latent = tn(hid[...].reshape(8 * HS, 256), w[...].reshape(8 * HS, features))
    target = feats[...].astype(F32)
    target = target * lax.rsqrt(jnp.mean(target * target, axis=1, keepdims=True) + 1e-06)
    grad = target * (-weight / math.sqrt(features))
    r = lax.rsqrt(jnp.mean(latent * latent, axis=1, keepdims=True) + 1e-06)
    along = jnp.mean(grad * latent, axis=1, keepdims=True)
    grad_latent = (r * (grad - latent * (r * r * along))).astype(BF16)
    for head in range(8):
        part = w[head // 2, 2 * (head % 2) : 2 * (head % 2) + 2].reshape(HS, features)
        grad_hidden[head] = nt(part, grad_latent).astype(BF16)
        grad_proj[head // 2, 2 * (head % 2) : 2 * (head % 2) + 2] = (
            nn(hid[head], grad_latent).astype(BF16).reshape(2, 2, HS // 4, features)
        )


def spread(acc, meta, chain, m, term):
    pick = jnp.broadcast_to(meta[chain, m : m + 1, 0:BLK], (BLK, BLK))
    upper = term * pick
    acc[chain, 0:BLK, :] += term - upper
    acc[chain, BLK : 2 * BLK, :] += upper


def backward_view(i, qh, kh, vh, mh, probs, inverse, outs, gh, grad_q, acck, accv, ksel, vsel):
    gather_blocks(i, kh, mh, ksel)
    gather_blocks(i, vh, mh, vsel)
    q = qh[i]
    inv = inverse[i]
    g = gh[i]
    gf = g.astype(F32)
    center = jnp.sum(gf * outs[i].astype(F32), axis=0, keepdims=True)
    scaled = (gf * inv).astype(BF16)
    grad_qt = jnp.zeros((HS, 256), F32)
    for c in range(5):
        rows = slice(c * 256, c * 256 + 256)
        p = probs[i, rows, :]
        dp = nn(vsel[rows, :], g)
        ds = (p.astype(F32) * ((dp - center) * inv)).astype(BF16)
        dk = nn(ds, q) * SCALE
        dv = nt(p, scaled)
        grad_qt = grad_qt + tn(ksel[rows, :], ds)
        if c == 0:
            acck[i + 4] += dk
            accv[i + 4] += dv
        else:
            for b in range(2):
                m = 2 * (c - 1) + b
                half = slice(b * BLK, (b + 1) * BLK)
                spread(acck, mh, i + 4 + OFFSETS[m], m, dk[half])
                spread(accv, mh, i + 4 + OFFSETS[m], m, dv[half])
    grad_q[i] = (grad_qt * SCALE).T.astype(BF16)


def total_of(parts):
    total = parts[0].astype(F32)
    for part in parts[1:]:
        total = total + part.astype(F32)
    return total


def nearest(k):
    odd = k % 2
    return (odd * ((k + 1) // 2) + (1 - odd) * (8 - k // 2)) % 8


def whole_kernel(
    q,
    k,
    v,
    picks,
    masks,
    wshard,
    feats,
    ids,
    table,
    oq,
    ok,
    ov,
    grad_rows,
    meta,
    qh,
    kh,
    vh,
    mh,
    w,
    probs,
    inverse,
    outs,
    hid,
    grad_hidden,
    gh,
    g,
    c1,
    a,
    c2,
    b,
    c3,
    c,
    c4,
    d,
    grad_q,
    acck,
    accv,
    edgek,
    edgev,
    landk,
    landv,
    fullk,
    fullv,
    ksel,
    vsel,
    scores,
    ls,
    ss,
    rs,
    hs,
    hr,
    ws,
    wr,
    os,
    ors,
    gs,
    gr,
    ps,
    pr,
    qs,
    qr,
    es,
    er,
    fs,
    fr,
):
    x, z = place()
    y = lax.axis_index("row")
    core = lax.axis_index("dp")
    root = 2 * y + core
    is_root = z == root
    other = {"dp": 1 - core}
    xs = [(x + n) % 4 for n in range(1, 4)]
    ys = [(y + n) % 4 for n in range(1, 4)]
    turns = [(dy, dc) for dy in range(4) for dc in range(2) if (dy, dc) != (0, 0)]
    column = [{"row": (y + dy) % 4, "dp": (core + dc) % 2} for dy, dc in turns]
    greet(z_peers() + [at_view(n, z) for n in xs] + column)

    def remote(src, dst, send_sem, recv_sem, device):
        return pltpu.make_async_remote_copy(src, dst, send_sem, recv_sem, device, MESH)

    def columns(h):
        return pl.ds(pl.multiple_of(h * HS, HS), HS)

    def pieces(target, n):
        cols = columns(target)
        return (
            (meta, mh.at[z + 4]),
            (k.at[:, cols], kh.at[z + 4]),
            (v.at[:, cols], vh.at[z + 4]),
            (q.at[:, cols], qh.at[z]),
        )[n]

    def scatter(n, dist):
        target = (z + dist) % 8
        src, dst = pieces(target, n)
        return remote(src, dst, ss.at[n, dist], rs.at[n, dist], at_view(x, target))

    def halo(n, dist):
        origin = (z + 8 - dist) % 8
        buf = (mh, kh, vh)[n]
        return remote(
            buf.at[origin + 4],
            buf.at[(origin + 12) % 16],
            hs.at[n, dist],
            hr.at[n, origin],
            at_view((x + 3 - 2 * (origin // 4)) % 4, z),
        )

    mine = w.at[x, y, core]
    mine_y = w.at[:, y, core]
    mine_c = w.at[:, :, core]
    fan = [remote(mine, mine, ws.at[n], wr.at[0], at_view(x, (z + n + 1) % 8)) for n in range(7)]
    along_x = [
        remote(mine, mine, ws.at[7 + n], wr.at[1 + n], at_view(t, z)) for n, t in enumerate(xs)
    ]
    along_y = [
        remote(mine_y, mine_y, ws.at[10 + n], wr.at[4 + n], {"row": t}) for n, t in enumerate(ys)
    ]
    along_c = remote(mine_c, mine_c, ws.at[13], wr.at[7], other)
    own = [pltpu.make_async_copy(*pieces(z, n), ls.at[n]) for n in range(4)]
    for m in range(8):
        for n, flag in enumerate((picks[0, m], masks[0, m], masks[1, m])):
            meta[m : m + 1, n * BLK : (n + 1) * BLK] = jnp.full((1, BLK), flag.astype(F32))

    @pl.when(is_root)
    def _():
        copy = pltpu.make_async_copy(wshard, mine, ls.at[4])
        copy.start()
        copy.wait()
        for s in fan:
            s.start()

    for n in range(2):
        own[n].start()
        for dist in ORDER:
            scatter(n, dist).start()

    @pl.when(jnp.logical_not(is_root))
    def _():
        fan[0].wait_recv()

    for s in along_x:
        s.start()
    for n in range(2, 4):
        own[n].start()
        for dist in ORDER if n < 3 else NEAR:
            scatter(n, dist).start()
    for n in range(3):
        own[n].wait()
        halo(n, 0).start()

    def pass_on(n):
        @pl.loop(1, 8)
        def _(turn):
            dist = nearest(turn)
            scatter(n, dist).wait_recv()
            halo(n, dist).start()

    pass_on(0)
    pass_on(1)
    for s in along_x:
        s.wait()
    for s in along_y:
        s.start()
    pass_on(2)
    for s in along_y:
        s.wait()
    along_c.start()

    @pl.when(is_root)
    def _():
        for s in fan:
            s.wait_send()

    @pl.loop(0, 8)
    def _(dist):
        for n in range(3):
            halo(n, dist).wait()

    def give_hidden(dist):
        target = (z + 8 - dist) % 8
        return remote(
            outs.at[target], hid.at[z], os.at[dist], ors.at[dist], at_view(x, target)
        )

    own[3].wait()

    @pl.loop(0, 8)
    def _(turn):
        dist = nearest(turn)
        view = (z + 8 - dist) % 8

        @pl.when(turn > 0)
        def _():
            scatter(3, dist).wait_recv()

        forward_view(view, qh, kh, vh, mh, probs, inverse, outs, ksel, vsel, scores)

        @pl.when(turn > 0)
        def _():
            give_hidden(dist).start()

    hid[z] = outs[z]

    @pl.loop(1, 8)
    def _(dist):
        for n in range(4):
            scatter(n, dist).wait_send()
        give_hidden(dist).wait()

    along_c.wait()
    project(hid, w, feats, table[ids[0, 0]], grad_hidden, g)

    def give_grad(dist):
        target = (z + dist) % 8
        return remote(
            grad_hidden.at[target], gh.at[z], gs.at[dist], gr.at[dist], at_view(x, target)
        )

    for dist in NEAR:
        give_grad(dist).start()
    gh[z] = grad_hidden[z]
    acck[...] = jnp.zeros_like(acck)
    accv[...] = jnp.zeros_like(accv)
    across = remote(g.at[:, :, 1 - core], c1, ps.at[0], pr.at[0], other)
    across.start()
    reduce_y = [
        remote(a.at[:, t], c2.at[n], ps.at[1 + n], pr.at[1 + n], {"row": t})
        for n, t in enumerate(ys)
    ]
    reduce_x = [
        remote(b.at[t], c3.at[n], ps.at[4 + n], pr.at[4 + n], at_view(t, z))
        for n, t in enumerate(xs)
    ]
    reduce_z = remote(c, c4.at[z], ps.at[7], pr.at[8 + z], at_view(x, root))
    down = [remote(d, d, ps.at[8 + n], pr.at[7], device) for n, device in enumerate(column)]

    def give_q(dist):
        target = (z + 8 - dist) % 8
        return remote(
            grad_q.at[target], oq.at[:, columns(z)], qs.at[dist], qr.at[dist], at_view(x, target)
        )

    @pl.loop(0, 8)
    def _(turn):
        dist = nearest(turn)
        view = (z + 8 - dist) % 8

        @pl.when(turn > 0)
        def _():
            give_grad(dist).wait_recv()

        backward_view(
            view, qh, kh, vh, mh, probs, inverse, outs, gh, grad_q, acck, accv, ksel, vsel
        )

        @pl.when(turn > 0)
        def _():
            give_q(dist).start()

        @pl.when(turn == 1)
        def _():
            across.wait()
            for i in range(4):
                for j in range(4):
                    a[i, j] = total_of([g[i, j, core], c1[i, j]]).astype(BF16)
            for s in reduce_y:
                s.start()

        @pl.when(turn == 5)
        def _():
            for s in reduce_y:
                s.wait()
            b[...] = total_of([a[:, y], c2[0], c2[1], c2[2]]).astype(BF16)
            for s in reduce_x:
                s.start()

        @pl.when(turn == 7)
        def _():
            for s in reduce_x:
                s.wait()
            c[...] = total_of([b[x], c3[0], c3[1], c3[2]]).astype(BF16)

            @pl.when(jnp.logical_not(is_root))
            def _():
                reduce_z.start()

    own_q = pltpu.make_async_copy(grad_q.at[z], oq.at[:, columns(z)], ls.at[0])
    own_q.start()

    def edge(n, dist):
        view = (z + dist) % 8
        src, dst = ((edgek, landk), (edgev, landv))[n]
        return remote(
            src.at[view],
            dst.at[view],
            es.at[n, dist],
            er.at[n, dist],
            at_view((x + 1 + 2 * (view // 4)) % 4, z),
        )

    def give_terms(n, dist):
        target = (z + dist) % 8
        src, dst = ((fullk, ok), (fullv, ov))[n]
        return remote(
            src.at[target], dst.at[:, columns(z)], fs.at[n, dist], fr.at[n, dist], at_view(x, target)
        )

    @pl.loop(1, 9)
    def _(turn):
        dist = nearest(turn % 8)
        view = (z + dist) % 8
        for n, (acc, buf) in enumerate(((acck, edgek), (accv, edgev))):
            buf[view] = acc[(view + 12) % 16].astype(BF16)
            edge(n, dist).start()

    @pl.loop(1, 9)
    def _(turn):
        dist = nearest(turn % 8)
        view = (z + dist) % 8
        for n, (acc, land, full) in enumerate(((acck, landk, fullk), (accv, landv, fullv))):
            edge(n, dist).wait_recv()
            full[view] = (acc[view + 4] + land[view].astype(F32)).astype(BF16)

            @pl.when(turn < 8)
            def _():
                give_terms(n, dist).start()

    own_k = pltpu.make_async_copy(fullk.at[z], ok.at[:, columns(z)], ls.at[1])
    own_v = pltpu.make_async_copy(fullv.at[z], ov.at[:, columns(z)], ls.at[2])
    own_k.start()
    own_v.start()

    @pl.when(jnp.logical_not(is_root))
    def _():
        reduce_z.wait_send()
        down[0].wait_recv()

    @pl.when(is_root)
    def _():
        c4[z] = c[...]
        for n in range(1, 8):
            origin = (z + n) % 8
            remote(c, c4.at[origin], ps.at[7], pr.at[8 + origin], at_view(x, origin)).wait_recv()
        d[...] = total_of([c4[n] for n in range(8)]).astype(BF16)
        for s in down:
            s.start()
        for s in down:
            s.wait_send()

    grad_rows[...] = d[...].astype(F32)

    @pl.loop(1, 8)
    def _(dist):
        give_grad(dist).wait_send()
        give_q(dist).wait()
        for n in range(2):
            give_terms(n, dist).wait()

    @pl.loop(0, 8)
    def _(dist):
        for n in range(2):
            edge(n, dist).wait_send()

    own_q.wait()
    own_k.wait()
    own_v.wait()


def deliver(*refs):
    sources, targets, stages, came, went = refs[:4], refs[4:8], refs[8:12], refs[12], refs[13]
    into = [
        pltpu.make_async_copy(src, stage, came.at[n])
        for n, (src, stage) in enumerate(zip(sources, stages))
    ]
    onto = [
        pltpu.make_async_copy(stage, dst, went.at[n])
        for n, (stage, dst) in enumerate(zip(stages, targets))
    ]
    for copy in into:
        copy.start()
    for first, second in zip(into, onto):
        first.wait()
        second.start()
    for copy in onto:
        copy.wait()


def local(
    queries,
    key_tokens,
    values,
    encoder_feats,
    proj_weight,
    pick_blocks,
    pair_mask,
    step_ids,
    step_weight,
):
    dma = pltpu.SemaphoreType.DMA
    rows, width = queries.shape[2:]
    features = encoder_feats.shape[3]
    keys = 5 * 256
    shard = (width // 32, features)
    smem = pl.BlockSpec(memory_space=pltpu.SMEM)
    whole = struct((rows, width), BF16)
    head = pltpu.VMEM((8, rows, HS), BF16)
    chain = pltpu.VMEM((16, rows, HS), BF16)
    turned = pltpu.VMEM((8, HS, rows), BF16)
    shapes = [whole, whole, whole, struct(shard, F32)]
    results = pl.pallas_call(
        whole_kernel,
        out_shape=shapes,
        in_specs=[ANY] * 3 + [smem] * 2 + [ANY, VMEM] + [smem] * 2,
        out_specs=[ANY] * 3 + [VMEM],
        scratch_shapes=[
            pltpu.VMEM((8, 3 * BLK), F32),
            head,
            chain,
            chain,
            pltpu.VMEM((16, 8, 3 * BLK), F32),
            pltpu.VMEM((4, 4, 2) + shard, BF16),
            pltpu.VMEM((8, keys, rows), BF16),
            pltpu.VMEM((8, 1, rows), F32),
            turned,
            turned,
            turned,
            turned,
            pltpu.VMEM((4, 4, 2) + shard, BF16),
            pltpu.VMEM((4, 4) + shard, BF16),
            pltpu.VMEM((4, 4) + shard, BF16),
            pltpu.VMEM((3, 4) + shard, BF16),
            pltpu.VMEM((4,) + shard, BF16),
            pltpu.VMEM((3,) + shard, BF16),
            pltpu.VMEM(shard, BF16),
            pltpu.VMEM((8,) + shard, BF16),
            pltpu.VMEM(shard, BF16),
            head,
            pltpu.VMEM((16, rows, HS), F32),
            pltpu.VMEM((16, rows, HS), F32),
            head,
            head,
            head,
            head,
            head,
            head,
            pltpu.VMEM((keys, HS), BF16),
            pltpu.VMEM((keys, HS), BF16),
            pltpu.VMEM((keys, rows), F32),
            dma((5,)),
            dma((4, 8)),
            dma((4, 8)),
            dma((3, 8)),
            dma((3, 8)),
            dma((14,)),
            dma((8,)),
            dma((8,)),
            dma((8,)),
            dma((8,)),
            dma((8,)),
            dma((16,)),
            dma((16,)),
            dma((8,)),
            dma((8,)),
            dma((2, 8)),
            dma((2, 8)),
            dma((2, 8)),
            dma((2, 8)),
        ],
        compiler_params=remote_params(1),
        name="whole",
    )(
        queries[0, 0],
        key_tokens[0, 0],
        values[0, 0],
        pick_blocks[0, 0],
        pair_mask[0, 0],
        proj_weight,
        encoder_feats[0, 0],
        step_ids,
        step_weight,
    )
    gq, gk, gv, grad_rows = pl.pallas_call(
        deliver,
        out_shape=shapes,
        in_specs=[ANY] * 4,
        out_specs=[ANY] * 4,
        scratch_shapes=[pltpu.VMEM(part.shape, part.dtype) for part in shapes]
        + [dma((4,)), dma((4,))],
        compiler_params=pltpu.CompilerParams(vmem_limit_bytes=LIMIT),
        name="deliver",
    )(*results)
    return gq[None, None], gk[None, None], gv[None, None], grad_rows


def solution(mesh):
    band = P("dp", "view", "row", None)
    return jax.shard_map(
        local,
        mesh=mesh,
        in_specs=(
            band,
            band,
            band,
            band,
            P("view", None),
            band,
            band,
            P("dp", "view"),
            P(),
        ),
        out_specs=(band, band, band, P("view", None)),
        check_vma=False,
    )
```

```python
import functools
import math

import jax
import jax.numpy as jnp
from jax import lax
from jax.experimental import pallas as pl
from jax.experimental.pallas import tpu as pltpu
from jax.sharding import PartitionSpec as P

HS = 128
BLK = 128
MESH = pl.DeviceIdType.MESH
F32 = jnp.float32
BF16 = jnp.bfloat16
OFFSETS = (1, 2, 3, 4, -1, -2, -3, -4)
NEAR = (1, 7, 2, 6, 3, 5, 4)
SCALE = 1.0 / math.sqrt(HS)
SCALE2 = SCALE * math.log2(math.e)
VMEM = pl.BlockSpec(memory_space=pltpu.VMEM)
ANY = pl.BlockSpec(memory_space=pl.ANY)
LIMIT = 60 * 1024 * 1024


def nt(a, b):
    return lax.dot_general(a, b, (((1,), (1,)), ((), ())), preferred_element_type=F32)


def tn(a, b):
    return lax.dot_general(a, b, (((0,), (0,)), ((), ())), preferred_element_type=F32)


def nn(a, b):
    return jnp.dot(a, b, preferred_element_type=F32)


def place():
    view = lax.axis_index("view")
    return view // 8, view % 8


def at_view(x, z):
    return {"view": x * 8 + z}


def greet(devices):
    barrier = pltpu.get_barrier_semaphore()
    for device in devices:
        pl.semaphore_signal(barrier, inc=1, device_id=device, device_id_type=MESH)
    pl.semaphore_wait(barrier, len(devices))


def z_peers():
    x, z = place()
    return [at_view(x, (z + k) % 8) for k in range(1, 8)]


def x_pair():
    x, z = place()
    return [at_view((x + 1) % 4, z), at_view((x + 3) % 4, z)]


def struct(shape, dtype):
    return jax.ShapeDtypeStruct(shape, dtype)


def remote_params(number):
    return pltpu.CompilerParams(
        collective_id=number, has_side_effects=True, vmem_limit_bytes=LIMIT
    )


def picked(ref, meta, chain, m):
    pick = jnp.broadcast_to(meta[chain, m : m + 1, 0:BLK], (BLK, BLK)).astype(BF16)
    return ref[chain, 0:BLK, :] * (1.0 - pick).astype(BF16) + ref[chain, BLK : 2 * BLK, :] * pick


def gather_blocks(i, ref, meta, out):
    out[0 : 2 * BLK, :] = ref[i + 4]
    for m, offset in enumerate(OFFSETS):
        out[(m + 2) * BLK : (m + 3) * BLK, :] = picked(ref, meta, i + 4 + offset, m)


def forward_view(i, qh, kh, vh, mh, probs, inverse, outs, rowed, ksel, vsel, scores):
    gather_blocks(i, kh, mh, ksel)
    gather_blocks(i, vh, mh, vsel)
    q = qh[i]
    seen = mh[i + 4][:, BLK:] > 0.5
    largest = None
    for c in range(5):
        rows = slice(c * 256, c * 256 + 256)
        part = nt(ksel[rows, :], q)
        scores[rows, :] = part
        if c == 0:
            largest = jnp.max(part, axis=0, keepdims=True)
        else:
            for b in range(2):
                m = 2 * (c - 1) + b
                top = jnp.max(part[b * BLK : (b + 1) * BLK], axis=0, keepdims=True)
                largest = jnp.maximum(largest, jnp.where(seen[m : m + 1], top, -jnp.inf))
    base = largest * SCALE2
    total = jnp.zeros((1, 256), F32)
    hidden = jnp.zeros((HS, 256), F32)
    for c in range(5):
        halves = []
        for b in range(2):
            rows = slice(c * 256 + b * BLK, c * 256 + (b + 1) * BLK)
            if c == 0:
                shift = base
            else:
                m = 2 * (c - 1) + b
                shift = jnp.where(seen[m : m + 1], base, jnp.inf)
            p = jnp.exp2(scores[rows, :] * SCALE2 - shift)
            total = total + jnp.sum(p, axis=0, keepdims=True)
            p = p.astype(BF16)
            probs[i, rows, :] = p
            halves.append(p)
        rows = slice(c * 256, c * 256 + 256)
        hidden = hidden + tn(vsel[rows, :], jnp.concatenate(halves, axis=0))
    inv = 1.0 / total
    inverse[i] = inv
    hidden = hidden * inv
    outs[i] = hidden.astype(BF16)
    rowed[i] = hidden.T.astype(BF16)


def target_pull(feats, weight):
    target = feats.astype(F32)
    target = target * lax.rsqrt(jnp.mean(target * target, axis=1, keepdims=True) + 1e-06)
    return target * (-weight / math.sqrt(feats.shape[1]))


def loss_slope(latent, grad):
    r = lax.rsqrt(jnp.mean(latent * latent, axis=1, keepdims=True) + 1e-06)
    along = jnp.mean(grad * latent, axis=1, keepdims=True)
    return r * (grad - latent * (r * r * along))


def spread(acc, meta, chain, m, term):
    pick = jnp.broadcast_to(meta[chain, m : m + 1, 0:BLK], (BLK, BLK))
    upper = term * pick
    acc[chain, 0:BLK, :] += term - upper
    acc[chain, BLK : 2 * BLK, :] += upper


def backward_view(i, qh, kh, vh, mh, probs, inverse, outs, gh, grad_q, acck, accv, ksel, vsel):
    gather_blocks(i, kh, mh, ksel)
    gather_blocks(i, vh, mh, vsel)
    q = qh[i]
    inv = inverse[i]
    g = gh[i]
    gf = g.astype(F32)
    center = jnp.sum(gf * outs[i].astype(F32), axis=0, keepdims=True)
    scaled = (gf * inv).astype(BF16)
    grad_qt = jnp.zeros((HS, 256), F32)
    for c in range(5):
        rows = slice(c * 256, c * 256 + 256)
        p = probs[i, rows, :]
        dp = nn(vsel[rows, :], g)
        ds = (p.astype(F32) * ((dp - center) * inv)).astype(BF16)
        dk = nn(ds, q) * SCALE
        dv = nt(p, scaled)
        grad_qt = grad_qt + tn(ksel[rows, :], ds)
        if c == 0:
            acck[i + 4] += dk
            accv[i + 4] += dv
        else:
            for b in range(2):
                m = 2 * (c - 1) + b
                half = slice(b * BLK, (b + 1) * BLK)
                spread(acck, mh, i + 4 + OFFSETS[m], m, dk[half])
                spread(accv, mh, i + 4 + OFFSETS[m], m, dv[half])
    grad_q[i] = (grad_qt * SCALE).T.astype(BF16)


def total_of(parts):
    total = parts[0].astype(F32)
    for part in parts[1:]:
        total = total + part.astype(F32)
    return total


def nearest(k):
    odd = k % 2
    return (odd * ((k + 1) // 2) + (1 - odd) * (8 - k // 2)) % 8


def whole_kernel(
    q,
    k,
    v,
    picks,
    masks,
    wshard,
    feats,
    ids,
    table,
    oq,
    ok,
    ov,
    grad_rows,
    meta,
    qh,
    kh,
    vh,
    mh,
    w,
    probs,
    inverse,
    outs,
    rowed,
    hid,
    pull,
    grad_latent,
    grad_hidden,
    gh,
    g,
    c1,
    a,
    c2,
    b,
    c3,
    c,
    c4,
    d,
    grad_q,
    acck,
    accv,
    edgek,
    edgev,
    landk,
    landv,
    fullk,
    fullv,
    ksel,
    vsel,
    scores,
    ls,
    ss,
    rs,
    hs,
    hr,
    ws,
    wr,
    os,
    ors,
    gs,
    gr,
    ps,
    pr,
    qs,
    qr,
    es,
    er,
    fs,
    fr,
):
    x, z = place()
    y = lax.axis_index("row")
    core = lax.axis_index("dp")
    root = 2 * y + core
    is_root = z == root
    other = {"dp": 1 - core}
    xs = [(x + n) % 4 for n in range(1, 4)]
    ys = [(y + n) % 4 for n in range(1, 4)]
    turns = [(dy, dc) for dy in range(4) for dc in range(2) if (dy, dc) != (0, 0)]
    column = [{"row": (y + dy) % 4, "dp": (core + dc) % 2} for dy, dc in turns]
    mine = w.at[x, y, core]
    shard = pltpu.make_async_copy(wshard, mine, ls.at[4])

    @pl.when(is_root)
    def _():
        shard.start()

    for m in range(8):
        for n, flag in enumerate((picks[0, m], masks[0, m], masks[1, m])):
            meta[m : m + 1, n * BLK : (n + 1) * BLK] = jnp.full((1, BLK), flag.astype(F32))
    acck[...] = jnp.zeros_like(acck)
    accv[...] = jnp.zeros_like(accv)
    pull[...] = target_pull(feats[...], table[ids[0, 0]])

    @pl.when(is_root)
    def _():
        shard.wait()

    greet(z_peers() + [at_view(n, z) for n in xs] + column)

    def remote(src, dst, send_sem, recv_sem, device):
        return pltpu.make_async_remote_copy(src, dst, send_sem, recv_sem, device, MESH)

    def columns(h):
        return pl.ds(pl.multiple_of(h * HS, HS), HS)

    def pieces(target, n):
        cols = columns(target)
        return (
            (meta, mh.at[z + 4]),
            (k.at[:, cols], kh.at[z + 4]),
            (v.at[:, cols], vh.at[z + 4]),
            (q.at[:, cols], qh.at[z]),
        )[n]

    def scatter(n, dist):
        target = (z + dist) % 8
        src, dst = pieces(target, n)
        return remote(src, dst, ss.at[n, dist], rs.at[n, dist], at_view(x, target))

    def halo(n, dist):
        origin = (z + 8 - dist) % 8
        buf = (mh, kh, vh)[n]
        return remote(
            buf.at[origin + 4],
            buf.at[(origin + 12) % 16],
            hs.at[n, dist],
            hr.at[n, origin],
            at_view((x + 3 - 2 * (origin // 4)) % 4, z),
        )

    mine_y = w.at[:, y, core]
    mine_c = w.at[:, :, core]
    fan = [remote(mine, mine, ws.at[n], wr.at[0], at_view(x, (z + n + 1) % 8)) for n in range(7)]
    along_x = [
        remote(mine, mine, ws.at[7 + n], wr.at[1 + n], at_view(t, z)) for n, t in enumerate(xs)
    ]
    along_y = [
        remote(mine_y, mine_y, ws.at[10 + n], wr.at[4 + n], {"row": t}) for n, t in enumerate(ys)
    ]
    along_c = remote(mine_c, mine_c, ws.at[13], wr.at[7], other)
    own = [pltpu.make_async_copy(*pieces(z, n), ls.at[n]) for n in range(4)]
    @pl.when(is_root)
    def _():
        for s in fan:
            s.start()

    for n in range(2):
        own[n].start()
        for dist in NEAR:
            scatter(n, dist).start()

    @pl.when(jnp.logical_not(is_root))
    def _():
        fan[0].wait_recv()

    for s in along_x:
        s.start()
    for n in range(2, 4):
        own[n].start()
    for dist in NEAR:
        scatter(2, dist).start()
    for n in range(3):
        own[n].wait()
        halo(n, 0).start()

    def pass_on(n):
        @pl.loop(1, 8)
        def _(turn):
            dist = nearest(turn)
            scatter(n, dist).wait_recv()
            halo(n, dist).start()
            if n == 2:
                scatter(3, dist).start()

    pass_on(0)
    pass_on(1)
    for s in along_x:
        s.wait()
    for s in along_y:
        s.start()
    pass_on(2)
    for s in along_y:
        s.wait()
    along_c.start()

    @pl.when(is_root)
    def _():
        for s in fan:
            s.wait_send()

    @pl.loop(0, 8)
    def _(dist):
        for n in range(3):
            halo(n, dist).wait()

    def give_hidden(dist):
        target = (z + 8 - dist) % 8
        return remote(
            rowed.at[target], hid.at[:, columns(z)], os.at[dist], ors.at[dist], at_view(x, target)
        )

    own[3].wait()

    @pl.loop(0, 8)
    def _(turn):
        dist = nearest(turn)
        view = (z + 8 - dist) % 8

        @pl.when(turn > 0)
        def _():
            scatter(3, dist).wait_recv()

        forward_view(
            view, qh, kh, vh, mh, probs, inverse, outs, rowed, ksel, vsel, scores
        )

        @pl.when(turn > 0)
        def _():
            give_hidden(dist).start()

    hid[:, columns(z)] = rowed[z]

    @pl.loop(1, 8)
    def _(dist):
        for n in range(4):
            scatter(n, dist).wait_send()
        give_hidden(dist).wait()

    along_c.wait()
    features = feats.shape[1]
    latent = nn(hid[...], w[...].reshape(8 * HS, features))
    grad_latent[...] = loss_slope(latent, pull[...]).astype(BF16)

    def give_grad(dist):
        target = (z + dist) % 8
        return remote(
            grad_hidden.at[target], gh.at[z], gs.at[dist], gr.at[dist], at_view(x, target)
        )

    for dist in NEAR + (0,):
        head = (z + dist) % 8
        part = w[head // 2, pl.ds(2 * (head % 2), 2)].reshape(HS, features)
        piece = nt(part, grad_latent[...]).astype(BF16)
        if dist:
            grad_hidden[head] = piece
            give_grad(dist).start()
        else:
            gh[z] = piece
    for head in range(8):
        g[head // 2, 2 * (head % 2) : 2 * (head % 2) + 2] = (
            tn(hid[:, head * HS : (head + 1) * HS], grad_latent[...])
            .astype(BF16)
            .reshape(2, 2, HS // 4, features)
        )
    across = remote(g.at[:, :, 1 - core], c1, ps.at[0], pr.at[0], other)
    across.start()
    reduce_y = [
        remote(a.at[:, t], c2.at[n], ps.at[1 + n], pr.at[1 + n], {"row": t})
        for n, t in enumerate(ys)
    ]
    reduce_x = [
        remote(b.at[t], c3.at[n], ps.at[4 + n], pr.at[4 + n], at_view(t, z))
        for n, t in enumerate(xs)
    ]
    reduce_z = remote(c, c4.at[z], ps.at[7], pr.at[8 + z], at_view(x, root))
    down = [remote(d, d, ps.at[8 + n], pr.at[7], device) for n, device in enumerate(column)]

    def give_q(dist):
        target = (z + 8 - dist) % 8
        return remote(
            grad_q.at[target], oq.at[:, columns(z)], qs.at[dist], qr.at[dist], at_view(x, target)
        )

    @pl.loop(0, 8)
    def _(turn):
        dist = nearest(turn)
        view = (z + 8 - dist) % 8

        @pl.when(turn > 0)
        def _():
            give_grad(dist).wait_recv()

        backward_view(
            view, qh, kh, vh, mh, probs, inverse, outs, gh, grad_q, acck, accv, ksel, vsel
        )

        @pl.when(turn > 0)
        def _():
            give_q(dist).start()

        @pl.when(turn == 1)
        def _():
            across.wait()
            for i in range(4):
                for j in range(4):
                    a[i, j] = total_of([g[i, j, core], c1[i, j]]).astype(BF16)
            for s in reduce_y:
                s.start()

        @pl.when(turn == 6)
        def _():
            for s in reduce_y:
                s.wait()
            b[...] = total_of([a[:, y], c2[0], c2[1], c2[2]]).astype(BF16)
            for s in reduce_x:
                s.start()

    own_q = pltpu.make_async_copy(grad_q.at[z], oq.at[:, columns(z)], ls.at[0])
    own_q.start()

    def edge(n, dist):
        view = (z + dist) % 8
        src, dst = ((edgek, landk), (edgev, landv))[n]
        return remote(
            src.at[view],
            dst.at[view],
            es.at[n, dist],
            er.at[n, dist],
            at_view((x + 1 + 2 * (view // 4)) % 4, z),
        )

    def give_terms(n, dist):
        target = (z + dist) % 8
        src, dst = ((fullk, ok), (fullv, ov))[n]
        return remote(
            src.at[target], dst.at[:, columns(z)], fs.at[n, dist], fr.at[n, dist], at_view(x, target)
        )

    @pl.loop(1, 9)
    def _(turn):
        dist = nearest(turn % 8)
        view = (z + dist) % 8
        for n, (acc, buf) in enumerate(((acck, edgek), (accv, edgev))):
            buf[view] = acc[(view + 12) % 16].astype(BF16)
            edge(n, dist).start()

    for s in reduce_x:
        s.wait()
    c[...] = total_of([b[x], c3[0], c3[1], c3[2]]).astype(BF16)

    @pl.when(jnp.logical_not(is_root))
    def _():
        reduce_z.start()

    @pl.loop(1, 9)
    def _(turn):
        dist = nearest(turn % 8)
        view = (z + dist) % 8
        for n, (acc, land, full) in enumerate(((acck, landk, fullk), (accv, landv, fullv))):
            edge(n, dist).wait_recv()
            full[view] = (acc[view + 4] + land[view].astype(F32)).astype(BF16)

            @pl.when(turn < 8)
            def _():
                give_terms(n, dist).start()

    own_k = pltpu.make_async_copy(fullk.at[z], ok.at[:, columns(z)], ls.at[1])
    own_v = pltpu.make_async_copy(fullv.at[z], ov.at[:, columns(z)], ls.at[2])
    own_k.start()
    own_v.start()

    @pl.when(jnp.logical_not(is_root))
    def _():
        reduce_z.wait_send()
        down[0].wait_recv()

    @pl.when(is_root)
    def _():
        c4[z] = c[...]
        for n in range(1, 8):
            origin = (z + n) % 8
            remote(c, c4.at[origin], ps.at[7], pr.at[8 + origin], at_view(x, origin)).wait_recv()
        d[...] = total_of([c4[n] for n in range(8)]).astype(BF16)
        for s in down:
            s.start()
        for s in down:
            s.wait_send()

    grad_rows[...] = d[...].astype(F32)

    @pl.loop(1, 8)
    def _(dist):
        give_grad(dist).wait_send()
        give_q(dist).wait()
        for n in range(2):
            give_terms(n, dist).wait()

    @pl.loop(0, 8)
    def _(dist):
        for n in range(2):
            edge(n, dist).wait_send()

    own_q.wait()
    own_k.wait()
    own_v.wait()


def deliver(*refs):
    sources, targets, stages, came, went = refs[:4], refs[4:8], refs[8:12], refs[12], refs[13]
    into = [
        pltpu.make_async_copy(src, stage, came.at[n])
        for n, (src, stage) in enumerate(zip(sources, stages))
    ]
    onto = [
        pltpu.make_async_copy(stage, dst, went.at[n])
        for n, (stage, dst) in enumerate(zip(stages, targets))
    ]
    for copy in into:
        copy.start()
    for first, second in zip(into, onto):
        first.wait()
        second.start()
    for copy in onto:
        copy.wait()


def local(
    queries,
    key_tokens,
    values,
    encoder_feats,
    proj_weight,
    pick_blocks,
    pair_mask,
    step_ids,
    step_weight,
):
    dma = pltpu.SemaphoreType.DMA
    rows, width = queries.shape[2:]
    features = encoder_feats.shape[3]
    keys = 5 * 256
    shard = (width // 32, features)
    smem = pl.BlockSpec(memory_space=pltpu.SMEM)
    whole = struct((rows, width), BF16)
    head = pltpu.VMEM((8, rows, HS), BF16)
    chain = pltpu.VMEM((16, rows, HS), BF16)
    turned = pltpu.VMEM((8, HS, rows), BF16)
    shapes = [whole, whole, whole, struct(shard, F32)]
    results = pl.pallas_call(
        whole_kernel,
        out_shape=shapes,
        in_specs=[ANY] * 3 + [smem] * 2 + [ANY, VMEM] + [smem] * 2,
        out_specs=[ANY] * 3 + [VMEM],
        scratch_shapes=[
            pltpu.VMEM((8, 3 * BLK), F32),
            head,
            chain,
            chain,
            pltpu.VMEM((16, 8, 3 * BLK), F32),
            pltpu.VMEM((4, 4, 2) + shard, BF16),
            pltpu.VMEM((8, keys, rows), BF16),
            pltpu.VMEM((8, 1, rows), F32),
            turned,
            head,
            pltpu.VMEM((rows, width), BF16),
            pltpu.VMEM((rows, features), F32),
            pltpu.VMEM((rows, features), BF16),
            turned,
            turned,
            pltpu.VMEM((4, 4, 2) + shard, BF16),
            pltpu.VMEM((4, 4) + shard, BF16),
            pltpu.VMEM((4, 4) + shard, BF16),
            pltpu.VMEM((3, 4) + shard, BF16),
            pltpu.VMEM((4,) + shard, BF16),
            pltpu.VMEM((3,) + shard, BF16),
            pltpu.VMEM(shard, BF16),
            pltpu.VMEM((8,) + shard, BF16),
            pltpu.VMEM(shard, BF16),
            head,
            pltpu.VMEM((16, rows, HS), F32),
            pltpu.VMEM((16, rows, HS), F32),
            head,
            head,
            head,
            head,
            head,
            head,
            pltpu.VMEM((keys, HS), BF16),
            pltpu.VMEM((keys, HS), BF16),
            pltpu.VMEM((keys, rows), F32),
            dma((5,)),
            dma((4, 8)),
            dma((4, 8)),
            dma((3, 8)),
            dma((3, 8)),
            dma((14,)),
            dma((8,)),
            dma((8,)),
            dma((8,)),
            dma((8,)),
            dma((8,)),
            dma((16,)),
            dma((16,)),
            dma((8,)),
            dma((8,)),
            dma((2, 8)),
            dma((2, 8)),
            dma((2, 8)),
            dma((2, 8)),
        ],
        compiler_params=remote_params(1),
        name="whole",
    )(
        queries[0, 0],
        key_tokens[0, 0],
        values[0, 0],
        pick_blocks[0, 0],
        pair_mask[0, 0],
        proj_weight,
        encoder_feats[0, 0],
        step_ids,
        step_weight,
    )
    gq, gk, gv, grad_rows = pl.pallas_call(
        deliver,
        out_shape=shapes,
        in_specs=[ANY] * 4,
        out_specs=[ANY] * 4,
        scratch_shapes=[pltpu.VMEM(part.shape, part.dtype) for part in shapes]
        + [dma((4,)), dma((4,))],
        compiler_params=pltpu.CompilerParams(vmem_limit_bytes=LIMIT),
        name="deliver",
    )(*results)
    return gq[None, None], gk[None, None], gv[None, None], grad_rows


def solution(mesh):
    band = P("dp", "view", "row", None)
    return jax.shard_map(
        local,
        mesh=mesh,
        in_specs=(
            band,
            band,
            band,
            band,
            P("view", None),
            band,
            band,
            P("dp", "view"),
            P(),
        ),
        out_specs=(band, band, band, P("view", None)),
        check_vma=False,
    )
```

```python
import functools
import math

import jax
import jax.numpy as jnp
from jax import lax
from jax.experimental import pallas as pl
from jax.experimental.pallas import tpu as pltpu
from jax.sharding import PartitionSpec as P

HS = 128
BLK = 128
MESH = pl.DeviceIdType.MESH
F32 = jnp.float32
BF16 = jnp.bfloat16
OFFSETS = (1, 2, 3, 4, -1, -2, -3, -4)
NEAR = (1, 7, 2, 6, 3, 5, 4)
SCALE = 1.0 / math.sqrt(HS)
SCALE2 = SCALE * math.log2(math.e)
VMEM = pl.BlockSpec(memory_space=pltpu.VMEM)
ANY = pl.BlockSpec(memory_space=pl.ANY)
LIMIT = 60 * 1024 * 1024


def nt(a, b):
    return lax.dot_general(a, b, (((1,), (1,)), ((), ())), preferred_element_type=F32)


def tn(a, b):
    return lax.dot_general(a, b, (((0,), (0,)), ((), ())), preferred_element_type=F32)


def nn(a, b):
    return jnp.dot(a, b, preferred_element_type=F32)


def place():
    view = lax.axis_index("view")
    return view // 8, view % 8


def at_view(x, z):
    return {"view": x * 8 + z}


def greet(devices):
    barrier = pltpu.get_barrier_semaphore()
    for device in devices:
        pl.semaphore_signal(barrier, inc=1, device_id=device, device_id_type=MESH)
    pl.semaphore_wait(barrier, len(devices))


def z_peers():
    x, z = place()
    return [at_view(x, (z + k) % 8) for k in range(1, 8)]


def x_pair():
    x, z = place()
    return [at_view((x + 1) % 4, z), at_view((x + 3) % 4, z)]


def struct(shape, dtype):
    return jax.ShapeDtypeStruct(shape, dtype)


def remote_params(number):
    return pltpu.CompilerParams(
        collective_id=number, has_side_effects=True, vmem_limit_bytes=LIMIT
    )


def picked(ref, meta, chain, m):
    pick = jnp.broadcast_to(meta[chain, m : m + 1, 0:BLK], (BLK, BLK)).astype(BF16)
    return ref[chain, 0:BLK, :] * (1.0 - pick).astype(BF16) + ref[chain, BLK : 2 * BLK, :] * pick


def gather_blocks(i, ref, meta, out):
    out[0 : 2 * BLK, :] = ref[i + 4]
    for m, offset in enumerate(OFFSETS):
        out[(m + 2) * BLK : (m + 3) * BLK, :] = picked(ref, meta, i + 4 + offset, m)


def forward_view(i, qh, kh, vh, mh, probs, inverse, outs, rowed, ksel, vsel, scores):
    gather_blocks(i, kh, mh, ksel)
    gather_blocks(i, vh, mh, vsel)
    q = qh[i]
    seen = mh[i + 4][:, BLK:] > 0.5
    largest = None
    for c in range(5):
        rows = slice(c * 256, c * 256 + 256)
        part = nt(ksel[rows, :], q)
        scores[rows, :] = part
        if c == 0:
            largest = jnp.max(part, axis=0, keepdims=True)
        else:
            for b in range(2):
                m = 2 * (c - 1) + b
                top = jnp.max(part[b * BLK : (b + 1) * BLK], axis=0, keepdims=True)
                largest = jnp.maximum(largest, jnp.where(seen[m : m + 1], top, -jnp.inf))
    base = largest * SCALE2
    total = jnp.zeros((1, 256), F32)
    hidden = jnp.zeros((HS, 256), F32)
    for c in range(5):
        halves = []
        for b in range(2):
            rows = slice(c * 256 + b * BLK, c * 256 + (b + 1) * BLK)
            if c == 0:
                shift = base
            else:
                m = 2 * (c - 1) + b
                shift = jnp.where(seen[m : m + 1], base, jnp.inf)
            p = jnp.exp2(scores[rows, :] * SCALE2 - shift)
            total = total + jnp.sum(p, axis=0, keepdims=True)
            p = p.astype(BF16)
            probs[i, rows, :] = p
            halves.append(p)
        rows = slice(c * 256, c * 256 + 256)
        hidden = hidden + tn(vsel[rows, :], jnp.concatenate(halves, axis=0))
    inv = 1.0 / total
    inverse[i] = inv
    hidden = hidden * inv
    outs[i] = hidden.astype(BF16)
    rowed[i] = hidden.T.astype(BF16)


def target_pull(feats, weight):
    target = feats.astype(F32)
    target = target * lax.rsqrt(jnp.mean(target * target, axis=1, keepdims=True) + 1e-06)
    return target * (-weight / math.sqrt(feats.shape[1]))


def loss_slope(latent, grad):
    r = lax.rsqrt(jnp.mean(latent * latent, axis=1, keepdims=True) + 1e-06)
    along = jnp.mean(grad * latent, axis=1, keepdims=True)
    return r * (grad - latent * (r * r * along))


def spread(acc, meta, chain, m, term):
    pick = jnp.broadcast_to(meta[chain, m : m + 1, 0:BLK], (BLK, BLK))
    upper = term * pick
    acc[chain, 0:BLK, :] += term - upper
    acc[chain, BLK : 2 * BLK, :] += upper


def backward_view(i, qh, kh, vh, mh, probs, inverse, outs, gh, grad_q, acck, accv, ksel, vsel):
    gather_blocks(i, kh, mh, ksel)
    gather_blocks(i, vh, mh, vsel)
    q = qh[i]
    inv = inverse[i]
    g = gh[i]
    gf = g.astype(F32)
    center = jnp.sum(gf * outs[i].astype(F32), axis=0, keepdims=True)
    scaled = (gf * inv).astype(BF16)
    grad_qt = jnp.zeros((HS, 256), F32)
    for c in range(5):
        rows = slice(c * 256, c * 256 + 256)
        p = probs[i, rows, :]
        dp = nn(vsel[rows, :], g)
        ds = (p.astype(F32) * ((dp - center) * inv)).astype(BF16)
        dk = nn(ds, q) * SCALE
        dv = nt(p, scaled)
        grad_qt = grad_qt + tn(ksel[rows, :], ds)
        if c == 0:
            acck[i + 4] += dk
            accv[i + 4] += dv
        else:
            for b in range(2):
                m = 2 * (c - 1) + b
                half = slice(b * BLK, (b + 1) * BLK)
                spread(acck, mh, i + 4 + OFFSETS[m], m, dk[half])
                spread(accv, mh, i + 4 + OFFSETS[m], m, dv[half])
    grad_q[i] = (grad_qt * SCALE).T.astype(BF16)


def total_of(parts):
    total = parts[0].astype(F32)
    for part in parts[1:]:
        total = total + part.astype(F32)
    return total


def nearest(k):
    odd = k % 2
    return (odd * ((k + 1) // 2) + (1 - odd) * (8 - k // 2)) % 8


def whole_kernel(
    q,
    k,
    v,
    picks,
    masks,
    wshard,
    feats,
    ids,
    table,
    oq,
    ok,
    ov,
    grad_rows,
    meta,
    mraw,
    qh,
    kh,
    vh,
    mh,
    w,
    probs,
    inverse,
    outs,
    rowed,
    hid,
    pull,
    latent,
    grad_latent,
    grad_hidden,
    gh,
    g,
    c1,
    a,
    c2,
    b,
    c3,
    c,
    c4,
    d,
    grad_q,
    acck,
    accv,
    edgek,
    edgev,
    landk,
    landv,
    fullk,
    fullv,
    ksel,
    vsel,
    scores,
    ls,
    ss,
    rs,
    hs,
    hr,
    ws,
    wr,
    os,
    ors,
    gs,
    gr,
    ps,
    pr,
    qs,
    qr,
    es,
    er,
    fs,
    fr,
):
    x, z = place()
    y = lax.axis_index("row")
    core = lax.axis_index("dp")
    root = 2 * y + core
    is_root = z == root
    other = {"dp": 1 - core}
    xs = [(x + n) % 4 for n in range(1, 4)]
    ys = [(y + n) % 4 for n in range(1, 4)]
    turns = [(dy, dc) for dy in range(4) for dc in range(2) if (dy, dc) != (0, 0)]
    column = [{"row": (y + dy) % 4, "dp": (core + dc) % 2} for dy, dc in turns]
    mine = w.at[x, y, core]
    shard = pltpu.make_async_copy(wshard, mine, ls.at[4])

    @pl.when(is_root)
    def _():
        shard.start()

    lane = lax.broadcasted_iota(jnp.int32, (1, BLK), 1)
    for m in range(8):
        flags = jnp.where(lane == 0, picks[0, m], jnp.where(lane == 1, masks[0, m], masks[1, m]))
        meta[m : m + 1, :] = flags.astype(F32)
    acck[...] = jnp.zeros_like(acck)
    accv[...] = jnp.zeros_like(accv)
    pull[...] = target_pull(feats[...], table[ids[0, 0]])

    @pl.when(is_root)
    def _():
        shard.wait()

    greet(z_peers() + [at_view(n, z) for n in xs] + column)

    def remote(src, dst, send_sem, recv_sem, device):
        return pltpu.make_async_remote_copy(src, dst, send_sem, recv_sem, device, MESH)

    def columns(h):
        return pl.ds(pl.multiple_of(h * HS, HS), HS)

    def pieces(target, n):
        cols = columns(target)
        return (
            (meta, mraw.at[z + 4]),
            (k.at[:, cols], kh.at[z + 4]),
            (v.at[:, cols], vh.at[z + 4]),
            (q.at[:, cols], qh.at[z]),
        )[n]

    def scatter(n, dist):
        target = (z + dist) % 8
        src, dst = pieces(target, n)
        return remote(src, dst, ss.at[n, dist], rs.at[n, dist], at_view(x, target))

    def halo(n, dist):
        origin = (z + 8 - dist) % 8
        buf = (mraw, kh, vh)[n]
        return remote(
            buf.at[origin + 4],
            buf.at[(origin + 12) % 16],
            hs.at[n, dist],
            hr.at[n, origin],
            at_view((x + 3 - 2 * (origin // 4)) % 4, z),
        )

    mine_y = w.at[:, y, core]
    mine_c = w.at[:, :, core]
    fan = [remote(mine, mine, ws.at[n], wr.at[0], at_view(x, (z + n + 1) % 8)) for n in range(7)]
    along_x = [
        remote(mine, mine, ws.at[7 + n], wr.at[1 + n], at_view(t, z)) for n, t in enumerate(xs)
    ]
    along_y = [
        remote(mine_y, mine_y, ws.at[10 + n], wr.at[4 + n], {"row": t}) for n, t in enumerate(ys)
    ]
    along_c = remote(mine_c, mine_c, ws.at[13], wr.at[7], other)
    own = [pltpu.make_async_copy(*pieces(z, n), ls.at[n]) for n in range(4)]
    @pl.when(is_root)
    def _():
        for s in fan:
            s.start()

    for n in range(2):
        own[n].start()
        for dist in NEAR:
            scatter(n, dist).start()

    @pl.when(jnp.logical_not(is_root))
    def _():
        fan[0].wait_recv()

    for s in along_x:
        s.start()
    for n in range(2, 4):
        own[n].start()
    for dist in NEAR:
        scatter(2, dist).start()
    for n in range(3):
        own[n].wait()
        halo(n, 0).start()

    def pass_on(n):
        @pl.loop(1, 8)
        def _(turn):
            dist = nearest(turn)
            scatter(n, dist).wait_recv()
            halo(n, dist).start()
            if n == 2:
                scatter(3, dist).start()

    pass_on(0)
    pass_on(1)
    for s in along_x:
        s.wait()
    for s in along_y:
        s.start()
    pass_on(2)
    for s in along_y:
        s.wait()
    along_c.start()

    @pl.when(is_root)
    def _():
        for s in fan:
            s.wait_send()

    @pl.loop(0, 8)
    def _(dist):
        for n in range(3):
            halo(n, dist).wait()

    @pl.loop(0, 16)
    def _(chain):
        for n in range(3):
            mh[chain, :, n * BLK : (n + 1) * BLK] = jnp.broadcast_to(
                mraw[chain][:, n : n + 1], (8, BLK)
            )

    def give_hidden(dist):
        target = (z + 8 - dist) % 8
        return remote(
            rowed.at[target], hid.at[:, columns(z)], os.at[dist], ors.at[dist], at_view(x, target)
        )

    own[3].wait()

    @pl.loop(0, 8)
    def _(turn):
        dist = nearest(turn)
        view = (z + 8 - dist) % 8

        @pl.when(turn > 0)
        def _():
            scatter(3, dist).wait_recv()

        forward_view(
            view, qh, kh, vh, mh, probs, inverse, outs, rowed, ksel, vsel, scores
        )

        @pl.when(turn > 0)
        def _():
            give_hidden(dist).start()

    @pl.loop(1, 8)
    def _(dist):
        for n in range(4):
            scatter(n, dist).wait_send()

    along_c.wait()
    features = feats.shape[1]

    def part_of(head):
        return w[head // 2, pl.ds(2 * (head % 2), 2)].reshape(HS, features)

    latent[...] = nn(rowed[z], part_of(z))

    @pl.loop(1, 8)
    def _(turn):
        dist = nearest(turn)
        give_hidden(dist).wait()
        head = (z + dist) % 8
        latent[...] += nn(hid[:, columns(head)], part_of(head))

    hid[:, columns(z)] = rowed[z]
    grad_latent[...] = loss_slope(latent[...], pull[...]).astype(BF16)

    def give_grad(dist):
        target = (z + dist) % 8
        return remote(
            grad_hidden.at[target], gh.at[z], gs.at[dist], gr.at[dist], at_view(x, target)
        )

    for dist in NEAR + (0,):
        head = (z + dist) % 8
        piece = nt(part_of(head), grad_latent[...]).astype(BF16)
        if dist:
            grad_hidden[head] = piece
            give_grad(dist).start()
        else:
            gh[z] = piece
    for head in range(8):
        g[head // 2, 2 * (head % 2) : 2 * (head % 2) + 2] = (
            tn(hid[:, head * HS : (head + 1) * HS], grad_latent[...])
            .astype(BF16)
            .reshape(2, 2, HS // 4, features)
        )
    across = remote(g.at[:, :, 1 - core], c1, ps.at[0], pr.at[0], other)
    across.start()
    reduce_y = [
        remote(a.at[:, t], c2.at[n], ps.at[1 + n], pr.at[1 + n], {"row": t})
        for n, t in enumerate(ys)
    ]
    reduce_x = [
        remote(b.at[t], c3.at[n], ps.at[4 + n], pr.at[4 + n], at_view(t, z))
        for n, t in enumerate(xs)
    ]
    reduce_z = remote(c, c4.at[z], ps.at[7], pr.at[8 + z], at_view(x, root))
    down = [remote(d, d, ps.at[8 + n], pr.at[7], device) for n, device in enumerate(column)]

    def give_q(dist):
        target = (z + 8 - dist) % 8
        return remote(
            grad_q.at[target], oq.at[:, columns(z)], qs.at[dist], qr.at[dist], at_view(x, target)
        )

    @pl.loop(0, 8)
    def _(turn):
        dist = nearest(turn)
        view = (z + 8 - dist) % 8

        @pl.when(turn > 0)
        def _():
            give_grad(dist).wait_recv()

        backward_view(
            view, qh, kh, vh, mh, probs, inverse, outs, gh, grad_q, acck, accv, ksel, vsel
        )

        @pl.when(turn > 0)
        def _():
            give_q(dist).start()

        @pl.when(turn == 1)
        def _():
            across.wait()
            for i in range(4):
                for j in range(4):
                    a[i, j] = total_of([g[i, j, core], c1[i, j]]).astype(BF16)
            for s in reduce_y:
                s.start()

        @pl.when(turn == 6)
        def _():
            for s in reduce_y:
                s.wait()
            b[...] = total_of([a[:, y], c2[0], c2[1], c2[2]]).astype(BF16)
            for s in reduce_x:
                s.start()

    own_q = pltpu.make_async_copy(grad_q.at[z], oq.at[:, columns(z)], ls.at[0])
    own_q.start()

    def edge(n, dist):
        view = (z + dist) % 8
        src, dst = ((edgek, landk), (edgev, landv))[n]
        return remote(
            src.at[view],
            dst.at[view],
            es.at[n, dist],
            er.at[n, dist],
            at_view((x + 1 + 2 * (view // 4)) % 4, z),
        )

    def give_terms(n, dist):
        target = (z + dist) % 8
        src, dst = ((fullk, ok), (fullv, ov))[n]
        return remote(
            src.at[target], dst.at[:, columns(z)], fs.at[n, dist], fr.at[n, dist], at_view(x, target)
        )

    @pl.loop(1, 9)
    def _(turn):
        dist = nearest(turn % 8)
        view = (z + dist) % 8
        for n, (acc, buf) in enumerate(((acck, edgek), (accv, edgev))):
            buf[view] = acc[(view + 12) % 16].astype(BF16)
            edge(n, dist).start()

    for s in reduce_x:
        s.wait()
    c[...] = total_of([b[x], c3[0], c3[1], c3[2]]).astype(BF16)

    @pl.when(jnp.logical_not(is_root))
    def _():
        reduce_z.start()

    @pl.loop(1, 9)
    def _(turn):
        dist = nearest(turn % 8)
        view = (z + dist) % 8
        for n, (acc, land, full) in enumerate(((acck, landk, fullk), (accv, landv, fullv))):
            edge(n, dist).wait_recv()
            full[view] = (acc[view + 4] + land[view].astype(F32)).astype(BF16)

            @pl.when(turn < 8)
            def _():
                give_terms(n, dist).start()

    own_k = pltpu.make_async_copy(fullk.at[z], ok.at[:, columns(z)], ls.at[1])
    own_v = pltpu.make_async_copy(fullv.at[z], ov.at[:, columns(z)], ls.at[2])
    own_k.start()
    own_v.start()

    @pl.when(jnp.logical_not(is_root))
    def _():
        reduce_z.wait_send()
        down[0].wait_recv()

    @pl.when(is_root)
    def _():
        c4[z] = c[...]
        for n in range(1, 8):
            origin = (z + n) % 8
            remote(c, c4.at[origin], ps.at[7], pr.at[8 + origin], at_view(x, origin)).wait_recv()
        d[...] = total_of([c4[n] for n in range(8)]).astype(BF16)
        for s in down:
            s.start()
        for s in down:
            s.wait_send()

    grad_rows[...] = d[...].astype(F32)

    @pl.loop(1, 8)
    def _(dist):
        give_grad(dist).wait_send()
        give_q(dist).wait()
        for n in range(2):
            give_terms(n, dist).wait()

    @pl.loop(0, 8)
    def _(dist):
        for n in range(2):
            edge(n, dist).wait_send()

    own_q.wait()
    own_k.wait()
    own_v.wait()


def deliver(*refs):
    sources, targets, stages, came, went = refs[:4], refs[4:8], refs[8:12], refs[12], refs[13]
    into = [
        pltpu.make_async_copy(src, stage, came.at[n])
        for n, (src, stage) in enumerate(zip(sources, stages))
    ]
    onto = [
        pltpu.make_async_copy(stage, dst, went.at[n])
        for n, (stage, dst) in enumerate(zip(stages, targets))
    ]
    for copy in into:
        copy.start()
    for first, second in zip(into, onto):
        first.wait()
        second.start()
    for copy in onto:
        copy.wait()


def local(
    queries,
    key_tokens,
    values,
    encoder_feats,
    proj_weight,
    pick_blocks,
    pair_mask,
    step_ids,
    step_weight,
):
    dma = pltpu.SemaphoreType.DMA
    rows, width = queries.shape[2:]
    features = encoder_feats.shape[3]
    keys = 5 * 256
    shard = (width // 32, features)
    smem = pl.BlockSpec(memory_space=pltpu.SMEM)
    whole = struct((rows, width), BF16)
    head = pltpu.VMEM((8, rows, HS), BF16)
    chain = pltpu.VMEM((16, rows, HS), BF16)
    turned = pltpu.VMEM((8, HS, rows), BF16)
    shapes = [whole, whole, whole, struct(shard, F32)]
    results = pl.pallas_call(
        whole_kernel,
        out_shape=shapes,
        in_specs=[ANY] * 3 + [smem] * 2 + [ANY, VMEM] + [smem] * 2,
        out_specs=[ANY] * 3 + [VMEM],
        scratch_shapes=[
            pltpu.VMEM((8, BLK), F32),
            pltpu.VMEM((16, 8, BLK), F32),
            head,
            chain,
            chain,
            pltpu.VMEM((16, 8, 3 * BLK), F32),
            pltpu.VMEM((4, 4, 2) + shard, BF16),
            pltpu.VMEM((8, keys, rows), BF16),
            pltpu.VMEM((8, 1, rows), F32),
            turned,
            head,
            pltpu.VMEM((rows, width), BF16),
            pltpu.VMEM((rows, features), F32),
            pltpu.VMEM((rows, features), F32),
            pltpu.VMEM((rows, features), BF16),
            turned,
            turned,
            pltpu.VMEM((4, 4, 2) + shard, BF16),
            pltpu.VMEM((4, 4) + shard, BF16),
            pltpu.VMEM((4, 4) + shard, BF16),
            pltpu.VMEM((3, 4) + shard, BF16),
            pltpu.VMEM((4,) + shard, BF16),
            pltpu.VMEM((3,) + shard, BF16),
            pltpu.VMEM(shard, BF16),
            pltpu.VMEM((8,) + shard, BF16),
            pltpu.VMEM(shard, BF16),
            head,
            pltpu.VMEM((16, rows, HS), F32),
            pltpu.VMEM((16, rows, HS), F32),
            head,
            head,
            head,
            head,
            head,
            head,
            pltpu.VMEM((keys, HS), BF16),
            pltpu.VMEM((keys, HS), BF16),
            pltpu.VMEM((keys, rows), F32),
            dma((5,)),
            dma((4, 8)),
            dma((4, 8)),
            dma((3, 8)),
            dma((3, 8)),
            dma((14,)),
            dma((8,)),
            dma((8,)),
            dma((8,)),
            dma((8,)),
            dma((8,)),
            dma((16,)),
            dma((16,)),
            dma((8,)),
            dma((8,)),
            dma((2, 8)),
            dma((2, 8)),
            dma((2, 8)),
            dma((2, 8)),
        ],
        compiler_params=remote_params(1),
        name="whole",
    )(
        queries[0, 0],
        key_tokens[0, 0],
        values[0, 0],
        pick_blocks[0, 0],
        pair_mask[0, 0],
        proj_weight,
        encoder_feats[0, 0],
        step_ids,
        step_weight,
    )
    gq, gk, gv, grad_rows = pl.pallas_call(
        deliver,
        out_shape=shapes,
        in_specs=[ANY] * 4,
        out_specs=[ANY] * 4,
        scratch_shapes=[pltpu.VMEM(part.shape, part.dtype) for part in shapes]
        + [dma((4,)), dma((4,))],
        compiler_params=pltpu.CompilerParams(vmem_limit_bytes=LIMIT),
        name="deliver",
    )(*results)
    return gq[None, None], gk[None, None], gv[None, None], grad_rows


def solution(mesh):
    band = P("dp", "view", "row", None)
    return jax.shard_map(
        local,
        mesh=mesh,
        in_specs=(
            band,
            band,
            band,
            band,
            P("view", None),
            band,
            band,
            P("dp", "view"),
            P(),
        ),
        out_specs=(band, band, band, P("view", None)),
        check_vma=False,
    )
```
